512 devices in a mesh: dp: 64 (over z_hi, y, core), fsdp: 8 (over z_lo, x).
Axes of the slice: x: 4, y: 8, z: 8 (z_hi: 4, z_lo: 2; z = z_hi * 2 + z_lo), core: 2. Of those that a mesh axis runs over, the one named last changes fastest.
Arguments:
- inputs: bfloat16 [768, 5120], P('dp', 'fsdp'), may hold values from -6 to 6
- upstream: bfloat16 [768, 5120], P('dp', 'fsdp'), may hold values from -6 to 6
- w_gate: bfloat16 [5120, 27648], P('fsdp', 'dp'), may hold values from -0.078125 to 0.078125
- w_up: bfloat16 [5120, 27648], P('fsdp', 'dp'), may hold values from -0.078125 to 0.078125
- w_down: bfloat16 [27648, 5120], P('dp', 'fsdp'), may hold values from -0.0390625 to 0.0390625
- lengths: int32 [64], replicated, may hold values from 1 to 12, as said below
- move_dest: int32 [64, 3], replicated, may hold values from 0 to 63, as said below
Outputs:
- grad_inputs: bfloat16 [384, 5120], P('dp', 'fsdp')
- grad_gate: bfloat16 [5120, 27648], P('fsdp', 'dp')
- grad_up: bfloat16 [5120, 27648], P('fsdp', 'dp')
- grad_down: bfloat16 [27648, 5120], P('dp', 'fsdp')
The draws below stay inside these ranges and needn't reach their ends.
Inputs may be any that keep to these rules, and one draw needn't show every extreme that they name: `lengths`: exactly a quarter of the learners have all 12 rows valid; every other learner has at most 1 block that hold valid rows. move_dest[l, m] is l itself exactly when block 3 + m of learner l holds no valid row; no learner sends two blocks to the same learner; a learner that receives k blocks sends none and has no valid row in its last k of the first 3 block slots; no learner receives more than 1 block.
All inputs are finite; a program needn't handle non-finite values.
Results may differ from the reference program's by a relative error of at most 0.0049.
Values may be sent and summed in bfloat16 or wider, within the bound.
No kernel may reach another device: no remote copies, remote signals or barrier semaphores. Data moves between devices by JAX's collectives and lax.ppermute only.
A program may use at most 64 MiB of HBM per device.

```python
import jax
import jax.numpy as jnp
from jax import lax

D = 5120
W = 27648
BLOCK = 2
HOLD_BLK = 3
CAP_ROWS = 12
ROWS = 768
N_DP = 64


def plan_draw(key):
    members = N_DP
    heavy = members // 4
    light = members - heavy
    slots_held = HOLD_BLK
    order = jax.random.permutation(jax.random.fold_in(key, 101), members).astype(jnp.int32)
    top_length = 2 * slots_held * BLOCK
    heavy_length = jnp.full((heavy,), top_length, jnp.int32)
    light_length = jax.random.randint(jax.random.fold_in(key, 103), (light,), 1, (slots_held - 2) * BLOCK + 1, dtype=jnp.int32)
    ranked_length = jnp.concatenate([heavy_length, light_length]).astype(jnp.int32)
    lengths = jnp.zeros((members,), jnp.int32).at[order].set(ranked_length)
    ranks = jnp.arange(members, dtype=jnp.int32)
    units = ranks[:, None] * slots_held + jnp.arange(slots_held, dtype=jnp.int32)[None, :]
    target = order[heavy + units % light]
    itself = jnp.broadcast_to(order[:, None], (members, slots_held))
    ranked_dest = jnp.where(ranks[:, None] < heavy, target, itself).astype(jnp.int32)
    move_dest = jnp.zeros((members, slots_held), jnp.int32).at[order].set(ranked_dest)
    return (lengths, move_dest)


def draw_lengths(key, part):
    shared = plan_draw(key)
    return shared[0]


def draw_move_dest(key, part):
    shared = plan_draw(key)
    return shared[1]


def levels(key, extent, cuts, low, high):
    factor_of, own = 1.0, jax.random.fold_in(key, 6)
    for axis_at, shards_of in cuts:
        steps = jnp.exp(jax.random.uniform(jax.random.fold_in(own, axis_at), (shards_of,), jnp.float32, low / len(cuts), high / len(cuts)))
        factor_of = factor_of * jnp.repeat(steps, extent[axis_at] // shards_of).reshape([-1 if axis == axis_at else 1 for axis in range(len(extent))])
    return factor_of


def bell_draw(stream_key, extent, scale, bound, split=(), kind=jnp.bfloat16):
    values = scale * jax.random.normal(stream_key, extent, jnp.float32)
    if split:
        values = values * levels(stream_key, extent, split, -0.22, 0.18)
    return jnp.clip(values, -bound, bound).astype(kind)


def setup_inputs(seed: int = 0) -> dict:
    seeds = jax.random.split(jax.random.key(seed), 8)
    inputs = bell_draw(seeds[0], (ROWS, D), 1.0, 6.0, ((0, 64), (1, 8)))
    upstream = bell_draw(seeds[1], (ROWS, D), 1.0, 6.0, ((0, 64), (1, 8)))
    w_gate = bell_draw(seeds[2], (D, W), D ** -0.5, 0.078125, ((0, 8), (1, 64)))
    w_up = bell_draw(seeds[3], (D, W), D ** -0.5, 0.078125, ((0, 8), (1, 64)))
    w_down = bell_draw(seeds[4], (W, D), W ** -0.5, 0.0390625, ((0, 64), (1, 8)))
    lengths = draw_lengths(jax.random.fold_in(seeds[7], 71), 0)
    move_dest = draw_move_dest(jax.random.fold_in(seeds[7], 71), 0)
    return {"inputs": inputs, "upstream": upstream, "w_gate": w_gate, "w_up": w_up, "w_down": w_down, "lengths": lengths, "move_dest": move_dest}


def reference(inputs, upstream, w_gate, w_up, w_down, lengths, move_dest):
    members = N_DP
    slots_held = HOLD_BLK
    valid_rows = (jnp.arange(CAP_ROWS, dtype=jnp.int32)[None, :] < lengths[:, None]).reshape(-1)[:, None]
    zero_value = jnp.zeros((), jnp.bfloat16)
    kept_in = jnp.where(valid_rows, inputs, zero_value)
    kept_up = jnp.where(valid_rows, upstream, zero_value)
    grad_scale = lax.rsqrt(jnp.sum(lengths).astype(jnp.float32))
    gate_value = jnp.dot(kept_in, w_gate, preferred_element_type=jnp.float32)
    up_value = jnp.dot(kept_in, w_up, preferred_element_type=jnp.float32)
    back_hidden = lax.dot_general(kept_up, w_down, (((1,), (1,)), ((), ())), preferred_element_type=jnp.float32)
    sigmoid_gate = jax.nn.sigmoid(gate_value)
    activated = gate_value * sigmoid_gate
    hidden = (activated * up_value).astype(jnp.bfloat16)
    grad_gate_hidden = (back_hidden * up_value * sigmoid_gate * (1.0 + gate_value * (1.0 - sigmoid_gate))).astype(jnp.bfloat16)
    grad_up_hidden = (back_hidden * activated).astype(jnp.bfloat16)
    contract_rows = (((0,), (0,)), ((), ()))
    gate_total = lax.dot_general(kept_in, grad_gate_hidden, contract_rows, preferred_element_type=jnp.float32)
    up_total = lax.dot_general(kept_in, grad_up_hidden, contract_rows, preferred_element_type=jnp.float32)
    down_total = lax.dot_general(hidden, kept_up, contract_rows, preferred_element_type=jnp.float32)
    contract_hidden = (((1,), (1,)), ((), ()))
    grad_rows = lax.dot_general(grad_gate_hidden, w_gate, contract_hidden, preferred_element_type=jnp.float32)
    grad_rows = grad_rows + lax.dot_general(grad_up_hidden, w_up, contract_hidden, preferred_element_type=jnp.float32)
    grad_rows = grad_rows.astype(jnp.bfloat16)
    learners = jnp.arange(members, dtype=jnp.int32)
    arrivals_hit = (move_dest[None, :, :] == learners[:, None, None]) & (learners[None, :, None] != learners[:, None, None])
    arriving = jnp.any(arrivals_hit, axis=2).astype(jnp.int32)
    which_block = lax.optimization_barrier(jnp.sum(jnp.where(arrivals_hit, jnp.arange(slots_held, dtype=jnp.int32)[None, None, :], 0), axis=2))
    arrival_rank = jnp.cumsum(arriving, axis=1) - arriving
    target_slot = slots_held - 1 - arrival_rank
    slot_match = (arriving[:, None, :] > 0) & (target_slot[:, None, :] == jnp.arange(slots_held, dtype=jnp.int32)[None, :, None])
    has_source = jnp.any(slot_match, axis=2)
    source_learner = lax.optimization_barrier(jnp.sum(jnp.where(slot_match, learners[None, None, :], 0), axis=2))
    source_block = lax.optimization_barrier(jnp.sum(jnp.where(slot_match, slots_held + which_block[:, None, :], 0), axis=2))
    own_slots = jnp.broadcast_to(jnp.arange(slots_held, dtype=jnp.int32)[None, :], (members, slots_held))
    own_learner = jnp.broadcast_to(learners[:, None], (members, slots_held))
    pick_learner = jnp.where(has_source, source_learner, own_learner).astype(jnp.int32)
    pick_block = jnp.where(has_source, source_block, own_slots).astype(jnp.int32)
    grad_blocks = grad_rows.reshape(members, 2 * slots_held, BLOCK, D)
    held = grad_blocks[pick_learner, pick_block].reshape(members * slots_held * BLOCK, D)
    return (held, (gate_total * grad_scale).astype(jnp.bfloat16), (up_total * grad_scale).astype(jnp.bfloat16), (down_total * grad_scale).astype(jnp.bfloat16))
```

```python
import jax
import jax.numpy as jnp
from jax import lax
from jax.sharding import PartitionSpec as P

LANES = 128
CORES = 2
Y_CHIPS = 8
Z_CHIPS = 4
BF16 = jnp.bfloat16
F32 = jnp.float32
SUM_TYPE = jnp.bfloat16


def dp_index(z, y, c):
    return (z * Y_CHIPS + y) * CORES + c


Z_GROUPS = [
    [dp_index(z, y, c) for z in range(Z_CHIPS)] for y in range(Y_CHIPS) for c in range(CORES)
]
Y_GROUPS = [
    [dp_index(z, y, c) for y in range(Y_CHIPS)] for z in range(Z_CHIPS) for c in range(CORES)
]


def exchange(x, axis, groups=None):
    return lax.all_to_all(x, axis, 0, 0, tiled=True, axis_index_groups=groups)


def copies(x, count):
    return jnp.broadcast_to(x[None], (count,) + x.shape)


def dense(x):
    n, rows, columns = x.shape
    tiles = columns // LANES
    x = x.reshape(n, rows, tiles, LANES).transpose(0, 2, 1, 3).reshape(n, tiles * rows, LANES)
    return jnp.pad(x, ((0, 0), (0, -(tiles * rows) % 16), (0, 0)))


def undense(x, rows):
    n, flat, _ = x.shape
    tiles = flat // rows
    x = x[:, : tiles * rows].reshape(n, tiles, rows, LANES).transpose(0, 2, 1, 3)
    return x.reshape(n, rows, tiles * LANES)


def body(inputs, upstream, w_gate, w_up, w_down, lengths, move_dest):
    members = lax.axis_size("dp")
    shards = lax.axis_size("fsdp")
    core = lax.axis_index("dp") % CORES
    capacity, features = inputs.shape
    hidden_units = w_gate.shape[1]
    heavy = members // 4
    rows = members * 4 + heavy * 2
    shard_rows = rows // shards
    width = 3 * hidden_units
    padding = -width % LANES

    is_full = lengths == capacity
    full_rank = jnp.cumsum(is_full.astype(jnp.int32)) - is_full
    learner = jnp.arange(members, dtype=jnp.int32)[:, None]
    row = jnp.arange(capacity, dtype=jnp.int32)[None, :]
    target = jnp.repeat(move_dest, 2, axis=1)
    target = jnp.concatenate([jnp.zeros_like(target), target], axis=1)
    place = jnp.where(
        row < 2,
        learner * 4 + row,
        jnp.where(
            row < 4,
            members * 4 + full_rank[:, None] * 2 + row - 2,
            jnp.where(row < 6, learner * 4 + row - 2, target * 4 + 2 + row % 2),
        ),
    )
    place = jnp.where(row < lengths[:, None], place, -1)
    place = place.reshape(Z_CHIPS, Y_CHIPS, CORES, capacity).transpose(2, 1, 0, 3)
    place = jnp.where(core == 0, place[0], place[1]).reshape(-1)
    pick = (jnp.arange(rows, dtype=jnp.int32)[:, None] == place[None, :]).astype(BF16)
    spread = (
        is_full[:, None] & (full_rank[:, None] == jnp.arange(heavy, dtype=jnp.int32)[None, :])
    ).astype(BF16)
    grad_scale = lax.rsqrt(jnp.sum(lengths).astype(F32))

    both = jnp.concatenate([inputs, upstream], axis=1)[None]
    with jax.named_scope("gather_z"):
        got = exchange(copies(dense(both)[0], Z_CHIPS), "dp", Z_GROUPS)
        got = undense(got, capacity).reshape(1, Z_CHIPS * capacity, 2 * features)
    with jax.named_scope("gather_y"):
        got = exchange(copies(dense(got)[0], Y_CHIPS), "dp", Y_GROUPS)
        got = undense(got, Z_CHIPS * capacity).reshape(-1, 2 * features)
    with jax.named_scope("gather_core"):
        mine = jnp.dot(pick, got, preferred_element_type=F32).astype(BF16)
        other = lax.ppermute(mine, "dp", [(i, i ^ 1) for i in range(members)])
        kept = mine + other
    kept_in, kept_up = kept[:, :features], kept[:, features:]

    w_in = jnp.concatenate([w_gate, w_up], axis=1)
    with jax.named_scope("partial_sums"):
        partial_in = jnp.dot(kept_in, w_in, preferred_element_type=F32)
        partial_back = lax.dot_general(
            kept_up, w_down, (((1,), (1,)), ((), ())), preferred_element_type=F32
        )
        partial = jnp.concatenate(
            [partial_in, partial_back, jnp.zeros((rows, padding), F32)], axis=1
        ).astype(SUM_TYPE)
        partial = dense(partial.reshape(shards, shard_rows, width + padding))
    with jax.named_scope("sum_features"):
        parts = exchange(partial, "fsdp")
        total = undense(jnp.sum(parts.astype(F32), axis=0, keepdims=True), shard_rows)[0]
    gate_value = total[:, :hidden_units]
    up_value = total[:, hidden_units : 2 * hidden_units]
    back_hidden = total[:, 2 * hidden_units : width]
    with jax.named_scope("activation"):
        sigmoid_gate = jax.nn.sigmoid(gate_value)
        activated = gate_value * sigmoid_gate
        hidden = (activated * up_value).astype(BF16)
        grad_gate_hidden = (
            back_hidden * up_value * sigmoid_gate * (1.0 + gate_value * (1.0 - sigmoid_gate))
        ).astype(BF16)
        grad_up_hidden = (back_hidden * activated).astype(BF16)
        shard = jnp.concatenate(
            [
                grad_gate_hidden,
                grad_up_hidden,
                hidden,
                jnp.zeros((shard_rows, padding), BF16),
            ],
            axis=1,
        )
    with jax.named_scope("gather_hidden"):
        all_hidden = exchange(copies(dense(shard[None])[0], shards), "fsdp")
        all_hidden = undense(all_hidden, shard_rows).reshape(rows, width + padding)
    grad_in_hidden = all_hidden[:, : 2 * hidden_units]
    hidden = all_hidden[:, 2 * hidden_units : width]

    with jax.named_scope("grad_rows"):
        grad_rows = lax.dot_general(
            grad_in_hidden, w_in, (((1,), (1,)), ((), ())), preferred_element_type=F32
        ).astype(BF16)
        outer = grad_rows[: members * 4].reshape(members, 2, 2, features)
        middle = jnp.einsum(
            "lh,htf->ltf",
            spread,
            grad_rows[members * 4 :].reshape(heavy, 2, features),
            preferred_element_type=F32,
        ).astype(BF16)
        slots = jnp.stack([outer[:, 0], middle, outer[:, 1]], axis=1).reshape(members, 6, features)
        arrived = exchange(dense(slots), "dp")
        grad_inputs = undense(jnp.sum(arrived.astype(F32), axis=0, keepdims=True), 6)[0].astype(BF16)

    contract_rows = (((0,), (0,)), ((), ()))
    with jax.named_scope("grad_weights"):
        in_total = lax.dot_general(
            kept_in, grad_in_hidden, contract_rows, preferred_element_type=F32
        )
        grad_in = (in_total * grad_scale).astype(BF16)
        down_total = lax.dot_general(hidden, kept_up, contract_rows, preferred_element_type=F32)
        grad_down = (down_total * grad_scale).astype(BF16)
    return (grad_inputs, grad_in[:, :hidden_units], grad_in[:, hidden_units:], grad_down)


def solution(mesh):
    in_specs = (
        P("dp", "fsdp"),
        P("dp", "fsdp"),
        P("fsdp", "dp"),
        P("fsdp", "dp"),
        P("dp", "fsdp"),
        P(),
        P(),
    )
    out_specs = (P("dp", "fsdp"), P("fsdp", "dp"), P("fsdp", "dp"), P("dp", "fsdp"))
    return jax.shard_map(body, mesh=mesh, in_specs=in_specs, out_specs=out_specs, check_vma=False)
```

```python
import jax
import jax.numpy as jnp
from jax import lax
from jax.sharding import PartitionSpec as P

LANES = 128
CORES = 2
BF16 = jnp.bfloat16
F32 = jnp.float32
SUM_TYPE = jnp.bfloat16


CORE_GROUPS = [
    [chip * CORES + core for chip in range(32)] for core in range(CORES)
]


def exchange(x, axis, groups=None):
    return lax.all_to_all(x, axis, 0, 0, tiled=True, axis_index_groups=groups)


def copies(x, count):
    return jnp.broadcast_to(x[None], (count,) + x.shape)


def dense(x):
    n, rows, columns = x.shape
    tiles = columns // LANES
    x = x.reshape(n, rows, tiles, LANES).transpose(0, 2, 1, 3).reshape(n, tiles * rows, LANES)
    return jnp.pad(x, ((0, 0), (0, -(tiles * rows) % 8), (0, 0)))


def undense(x, rows):
    n, flat, _ = x.shape
    tiles = flat // rows
    x = x[:, : tiles * rows].reshape(n, tiles, rows, LANES).transpose(0, 2, 1, 3)
    return x.reshape(n, rows, tiles * LANES)


def body(inputs, upstream, w_gate, w_up, w_down, lengths, move_dest):
    members = lax.axis_size("dp")
    shards = lax.axis_size("fsdp")
    core = lax.axis_index("dp") % CORES
    capacity, features = inputs.shape
    hidden_units = w_gate.shape[1]
    heavy = members // 4
    rows = members * 4 + heavy * 2
    shard_rows = rows // shards
    width = 3 * hidden_units
    padding = -width % LANES

    is_full = lengths == capacity
    full_rank = jnp.cumsum(is_full.astype(jnp.int32)) - is_full
    learner = jnp.arange(members, dtype=jnp.int32)[:, None]
    row = jnp.arange(capacity, dtype=jnp.int32)[None, :]
    target = jnp.repeat(move_dest, 2, axis=1)
    target = jnp.concatenate([jnp.zeros_like(target), target], axis=1)
    place = jnp.where(
        row < 2,
        learner * 4 + row,
        jnp.where(
            row < 4,
            members * 4 + full_rank[:, None] * 2 + row - 2,
            jnp.where(row < 6, learner * 4 + row - 2, target * 4 + 2 + row % 2),
        ),
    )
    place = jnp.where(row < lengths[:, None], place, -1)
    place = place.reshape(-1, CORES, capacity).transpose(1, 0, 2)
    place = jnp.where(core == 0, place[0], place[1]).reshape(-1)
    pick = (jnp.arange(rows, dtype=jnp.int32)[:, None] == place[None, :]).astype(BF16)
    spread = (
        is_full[:, None] & (full_rank[:, None] == jnp.arange(heavy, dtype=jnp.int32)[None, :])
    ).astype(BF16)
    grad_scale = lax.rsqrt(jnp.sum(lengths).astype(F32))

    both = jnp.concatenate([inputs, upstream], axis=1)[None]
    with jax.named_scope("gather_chips"):
        got = exchange(copies(dense(both)[0], members // CORES), "dp", CORE_GROUPS)
        got = undense(got, capacity).reshape(-1, 2 * features)
    with jax.named_scope("gather_core"):
        mine = jnp.dot(pick, got, preferred_element_type=F32).astype(BF16)
        other = lax.ppermute(mine, "dp", [(i, i ^ 1) for i in range(members)])
        kept = mine + other
    kept_in, kept_up = kept[:, :features], kept[:, features:]

    w_in = jnp.concatenate([w_gate, w_up], axis=1)
    with jax.named_scope("partial_sums"):
        partial_in = jnp.dot(kept_in, w_in, preferred_element_type=F32)
        partial_back = lax.dot_general(
            kept_up, w_down, (((1,), (1,)), ((), ())), preferred_element_type=F32
        )
        partial = jnp.concatenate(
            [partial_in, partial_back, jnp.zeros((rows, padding), F32)], axis=1
        ).astype(SUM_TYPE)
        partial = dense(partial.reshape(shards, shard_rows, width + padding))
    with jax.named_scope("sum_features"):
        parts = exchange(partial, "fsdp")
        total = undense(jnp.sum(parts.astype(F32), axis=0, keepdims=True), shard_rows)[0]
    gate_value = total[:, :hidden_units]
    up_value = total[:, hidden_units : 2 * hidden_units]
    back_hidden = total[:, 2 * hidden_units : width]
    with jax.named_scope("activation"):
        sigmoid_gate = jax.nn.sigmoid(gate_value)
        activated = gate_value * sigmoid_gate
        hidden = (activated * up_value).astype(BF16)
        grad_gate_hidden = (
            back_hidden * up_value * sigmoid_gate * (1.0 + gate_value * (1.0 - sigmoid_gate))
        ).astype(BF16)
        grad_up_hidden = (back_hidden * activated).astype(BF16)
        shard = jnp.concatenate(
            [
                grad_gate_hidden,
                grad_up_hidden,
                hidden,
                jnp.zeros((shard_rows, padding), BF16),
            ],
            axis=1,
        )
    with jax.named_scope("gather_hidden"):
        all_hidden = exchange(copies(dense(shard[None])[0], shards), "fsdp")
        all_hidden = undense(all_hidden, shard_rows).reshape(rows, width + padding)
    grad_in_hidden = all_hidden[:, : 2 * hidden_units]
    hidden = all_hidden[:, 2 * hidden_units : width]

    with jax.named_scope("grad_rows"):
        grad_rows = lax.dot_general(
            grad_in_hidden, w_in, (((1,), (1,)), ((), ())), preferred_element_type=F32
        ).astype(BF16)
        outer = grad_rows[: members * 4].reshape(members, 2, 2, features)
        middle = jnp.einsum(
            "lh,htf->ltf",
            spread,
            grad_rows[members * 4 :].reshape(heavy, 2, features),
            preferred_element_type=F32,
        ).astype(BF16)
        slots = jnp.stack([outer[:, 0], middle, outer[:, 1]], axis=1).reshape(members, 6, features)
        arrived = exchange(dense(slots), "dp")
        grad_inputs = undense(jnp.sum(arrived.astype(F32), axis=0, keepdims=True), 6)[0].astype(BF16)

    contract_rows = (((0,), (0,)), ((), ()))
    with jax.named_scope("grad_weights"):
        in_total = lax.dot_general(
            kept_in, grad_in_hidden, contract_rows, preferred_element_type=F32
        )
        grad_in = (in_total * grad_scale).astype(BF16)
        down_total = lax.dot_general(hidden, kept_up, contract_rows, preferred_element_type=F32)
        grad_down = (down_total * grad_scale).astype(BF16)
    return (grad_inputs, grad_in[:, :hidden_units], grad_in[:, hidden_units:], grad_down)


def solution(mesh):
    in_specs = (
        P("dp", "fsdp"),
        P("dp", "fsdp"),
        P("fsdp", "dp"),
        P("fsdp", "dp"),
        P("dp", "fsdp"),
        P(),
        P(),
    )
    out_specs = (P("dp", "fsdp"), P("fsdp", "dp"), P("fsdp", "dp"), P("dp", "fsdp"))
    return jax.shard_map(body, mesh=mesh, in_specs=in_specs, out_specs=out_specs, check_vma=False)
```

```python
import jax
import jax.numpy as jnp
from jax import lax
from jax.sharding import PartitionSpec as P

LANES = 128
CORES = 2
BF16 = jnp.bfloat16
F32 = jnp.float32
SUM_TYPE = jnp.bfloat16


Y_CHIPS = 8
Z_CHIPS = 4
SIDES = 2


def dp_index(z, y, core):
    return (z * Y_CHIPS + y % Y_CHIPS) * CORES + core


def moved(dy, dcore):
    return [
        (dp_index(z, y, core), dp_index(z, y + dy, core ^ dcore))
        for z in range(Z_CHIPS)
        for y in range(Y_CHIPS)
        for core in range(CORES)
    ]


SIDE_GROUPS = [
    [dp_index(z, y, core) for z in range(Z_CHIPS) for y in range(side, Y_CHIPS, SIDES)]
    for side in range(SIDES)
    for core in range(CORES)
]


def exchange(x, axis, groups=None):
    return lax.all_to_all(x, axis, 0, 0, tiled=True, axis_index_groups=groups)


def copies(x, count):
    return jnp.broadcast_to(x[None], (count,) + x.shape)


def dense(x):
    n, rows, columns = x.shape
    tiles = columns // LANES
    x = x.reshape(n, rows, tiles, LANES).transpose(0, 2, 1, 3).reshape(n, tiles * rows, LANES)
    return jnp.pad(x, ((0, 0), (0, -(tiles * rows) % 8), (0, 0)))


def undense(x, rows):
    n, flat, _ = x.shape
    tiles = flat // rows
    x = x[:, : tiles * rows].reshape(n, tiles, rows, LANES).transpose(0, 2, 1, 3)
    return x.reshape(n, rows, tiles * LANES)


def body(inputs, upstream, w_gate, w_up, w_down, lengths, move_dest):
    members = lax.axis_size("dp")
    shards = lax.axis_size("fsdp")
    core = lax.axis_index("dp") & 1
    side = (lax.axis_index("dp") >> 1) & 1
    capacity, features = inputs.shape
    hidden_units = w_gate.shape[1]
    heavy = members // 4
    rows = members * 4 + heavy * 2
    shard_rows = rows // shards
    width = 3 * hidden_units
    padding = -width % LANES

    is_full = lengths == capacity
    full_rank = jnp.cumsum(is_full.astype(jnp.int32)) - is_full
    learner = jnp.arange(members, dtype=jnp.int32)[:, None]
    row = jnp.arange(capacity, dtype=jnp.int32)[None, :]
    target = jnp.repeat(move_dest, 2, axis=1)
    target = jnp.concatenate([jnp.zeros_like(target), target], axis=1)
    place = jnp.where(
        row < 2,
        learner * 4 + row,
        jnp.where(
            row < 4,
            members * 4 + full_rank[:, None] * 2 + row - 2,
            jnp.where(row < 6, learner * 4 + row - 2, target * 4 + 2 + row % 2),
        ),
    )
    place = jnp.where(row < lengths[:, None], place, -1)
    place = place.reshape(Z_CHIPS, -1, SIDES, CORES, capacity).transpose(2, 3, 0, 1, 4)
    place = jnp.where(core == 0, place[:, 0], place[:, 1]).reshape(SIDES, -1)
    place = jnp.where(side == 0, place, place[::-1]).reshape(-1)
    pick = (jnp.arange(rows, dtype=jnp.int32)[:, None] == place[None, :]).astype(BF16)
    spread = (
        is_full[:, None] & (full_rank[:, None] == jnp.arange(heavy, dtype=jnp.int32)[None, :])
    ).astype(BF16)
    grad_scale = lax.rsqrt(jnp.sum(lengths).astype(F32))

    both = jnp.concatenate([inputs, upstream], axis=1)[None]
    with jax.named_scope("gather_side"):
        got = exchange(copies(dense(both)[0], members // (CORES * SIDES)), "dp", SIDE_GROUPS)
    with jax.named_scope("gather_neighbours"):
        half = got.shape[0] // 2
        first = lax.ppermute(got[:half], "dp", moved(-1, 0))
        second = lax.ppermute(got[half:], "dp", moved(1, 0))
        got = jnp.concatenate([got, first, second], axis=0)
        got = undense(got, capacity).reshape(-1, 2 * features)
    with jax.named_scope("gather_core"):
        mine = jnp.dot(pick, got, preferred_element_type=F32).astype(BF16)
        kept = mine + lax.ppermute(mine, "dp", moved(0, 1))
    kept_in, kept_up = kept[:, :features], kept[:, features:]

    w_in = jnp.concatenate([w_gate, w_up], axis=1)
    with jax.named_scope("partial_sums"):
        partial_in = jnp.dot(kept_in, w_in, preferred_element_type=F32)
        partial_back = lax.dot_general(
            kept_up, w_down, (((1,), (1,)), ((), ())), preferred_element_type=F32
        )
        partial = jnp.concatenate(
            [partial_in, partial_back, jnp.zeros((rows, padding), F32)], axis=1
        ).astype(SUM_TYPE)
        partial = dense(partial.reshape(shards, shard_rows, width + padding))
    with jax.named_scope("sum_features"):
        parts = exchange(partial, "fsdp")
        total = undense(jnp.sum(parts.astype(F32), axis=0, keepdims=True), shard_rows)[0]
    gate_value = total[:, :hidden_units]
    up_value = total[:, hidden_units : 2 * hidden_units]
    back_hidden = total[:, 2 * hidden_units : width]
    with jax.named_scope("activation"):
        sigmoid_gate = jax.nn.sigmoid(gate_value)
        activated = gate_value * sigmoid_gate
        hidden = (activated * up_value).astype(BF16)
        grad_gate_hidden = (
            back_hidden * up_value * sigmoid_gate * (1.0 + gate_value * (1.0 - sigmoid_gate))
        ).astype(BF16)
        grad_up_hidden = (back_hidden * activated).astype(BF16)
        shard = jnp.concatenate(
            [
                grad_gate_hidden,
                grad_up_hidden,
                hidden,
                jnp.zeros((shard_rows, padding), BF16),
            ],
            axis=1,
        )
    with jax.named_scope("gather_hidden"):
        all_hidden = exchange(copies(dense(shard[None])[0], shards), "fsdp")
        all_hidden = undense(all_hidden, shard_rows).reshape(rows, width + padding)
    grad_in_hidden = all_hidden[:, : 2 * hidden_units]
    hidden = all_hidden[:, 2 * hidden_units : width]

    with jax.named_scope("grad_rows"):
        grad_rows = lax.dot_general(
            grad_in_hidden, w_in, (((1,), (1,)), ((), ())), preferred_element_type=F32
        ).astype(BF16)
        outer = grad_rows[: members * 4].reshape(members, 2, 2, features)
        middle = jnp.einsum(
            "lh,htf->ltf",
            spread,
            grad_rows[members * 4 :].reshape(heavy, 2, features),
            preferred_element_type=F32,
        ).astype(BF16)
        slots = jnp.stack([outer[:, 0], middle, outer[:, 1]], axis=1).reshape(members, 6, features)
        arrived = exchange(dense(slots), "dp")
        grad_inputs = undense(jnp.sum(arrived.astype(F32), axis=0, keepdims=True), 6)[0].astype(BF16)

    contract_rows = (((0,), (0,)), ((), ()))
    with jax.named_scope("grad_weights"):
        in_total = lax.dot_general(
            kept_in, grad_in_hidden, contract_rows, preferred_element_type=F32
        )
        grad_in = (in_total * grad_scale).astype(BF16)
        down_total = lax.dot_general(hidden, kept_up, contract_rows, preferred_element_type=F32)
        grad_down = (down_total * grad_scale).astype(BF16)
    return (grad_inputs, grad_in[:, :hidden_units], grad_in[:, hidden_units:], grad_down)


def solution(mesh):
    in_specs = (
        P("dp", "fsdp"),
        P("dp", "fsdp"),
        P("fsdp", "dp"),
        P("fsdp", "dp"),
        P("dp", "fsdp"),
        P(),
        P(),
    )
    out_specs = (P("dp", "fsdp"), P("fsdp", "dp"), P("fsdp", "dp"), P("dp", "fsdp"))
    return jax.shard_map(body, mesh=mesh, in_specs=in_specs, out_specs=out_specs, check_vma=False)
```

```python
import jax
import jax.numpy as jnp
from jax import lax
from jax.sharding import PartitionSpec as P

LANES = 128
CORES = 2
BF16 = jnp.bfloat16
F32 = jnp.float32


CORE_GROUPS = [
    [chip * CORES + core for chip in range(32)] for core in range(CORES)
]


def exchange(x, axis, groups=None):
    return lax.all_to_all(x, axis, 0, 0, tiled=True, axis_index_groups=groups)


def copies(x, count):
    return jnp.broadcast_to(x[None], (count,) + x.shape)


def dense(x):
    n, rows, columns = x.shape
    tiles = columns // LANES
    x = x.reshape(n, rows, tiles, LANES).transpose(0, 2, 1, 3).reshape(n, tiles * rows, LANES)
    return jnp.pad(x, ((0, 0), (0, -(tiles * rows) % 8), (0, 0)))


def undense(x, rows):
    n, flat, _ = x.shape
    tiles = flat // rows
    x = x[:, : tiles * rows].reshape(n, tiles, rows, LANES).transpose(0, 2, 1, 3)
    return x.reshape(n, rows, tiles * LANES)


def pad_hidden(weights, axis):
    padding = [(0, 0), (0, 0)]
    padding[axis] = (0, -weights.shape[axis] % (4 * LANES))
    return jnp.pad(weights, padding)


def body(inputs, upstream, w_gate, w_up, w_down, lengths, move_dest):
    members = lax.axis_size("dp")
    shards = lax.axis_size("fsdp")
    core = lax.axis_index("dp") % CORES
    capacity, features = inputs.shape
    hidden_units = w_gate.shape[1]
    heavy = members // 4
    rows = members * 4 + heavy * 2

    is_full = lengths == capacity
    full_rank = jnp.cumsum(is_full.astype(jnp.int32)) - is_full
    learner = jnp.arange(members, dtype=jnp.int32)[:, None]
    row = jnp.arange(capacity, dtype=jnp.int32)[None, :]
    target = jnp.repeat(move_dest, 2, axis=1)
    target = jnp.concatenate([jnp.zeros_like(target), target], axis=1)
    place = jnp.where(
        row < 2,
        learner * 4 + row,
        jnp.where(
            row < 4,
            members * 4 + full_rank[:, None] * 2 + row - 2,
            jnp.where(row < 6, learner * 4 + row - 2, target * 4 + 2 + row % 2),
        ),
    )
    place = jnp.where(row < lengths[:, None], place, -1)
    place = place.reshape(-1, CORES, capacity).transpose(1, 0, 2)
    place = jnp.where(core == 0, place[0], place[1]).reshape(-1)
    pick = (jnp.arange(rows, dtype=jnp.int32)[:, None] == place[None, :]).astype(BF16)
    chips = jnp.arange(members // CORES, dtype=jnp.int32)[None, :] * CORES
    owner = chips + (jnp.arange(CORES, dtype=jnp.int32)[:, None] ^ core)
    middle = jnp.where(is_full, members * 4 + full_rank * 2, -2).reshape(-1, CORES).T
    middle = jnp.where(core == 0, middle, middle[::-1])
    source = jnp.stack([owner * 4, middle, owner * 4 + 2], axis=2)
    source = (source[..., None] + jnp.arange(2, dtype=jnp.int32)).reshape(-1)
    order = (source[:, None] == jnp.arange(rows, dtype=jnp.int32)[None, :]).astype(BF16)
    grad_scale = lax.rsqrt(jnp.sum(lengths).astype(F32))

    both = jnp.concatenate([inputs, upstream], axis=1)[None]
    with jax.named_scope("gather_chips"):
        got = exchange(copies(dense(both)[0], members // CORES), "dp", CORE_GROUPS)
        got = undense(got, capacity).reshape(-1, 2 * features)
    with jax.named_scope("gather_core"):
        mine = jnp.dot(pick, got, preferred_element_type=F32).astype(BF16)
        other = lax.ppermute(mine, "dp", [(i, i ^ 1) for i in range(members)])
        kept = mine + other
    kept_in, kept_up = kept[:, :features], kept[:, features:]

    with jax.named_scope("partial_sums"):
        w_in = jnp.concatenate([pad_hidden(w_gate, 1), pad_hidden(w_up, 1)], axis=1)
        w_back = pad_hidden(w_down, 0)
        padded = w_back.shape[0]
        partial_in = jnp.dot(kept_in, w_in, preferred_element_type=F32)
        partial_back = lax.dot_general(
            kept_up, w_back, (((1,), (1,)), ((), ())), preferred_element_type=F32
        )
        partial = jnp.concatenate([partial_in.astype(BF16), partial_back.astype(BF16)], axis=1)
        halves = shards * LANES // padded
        partial = partial.reshape(halves, rows // halves, 3, padded // LANES, LANES)
        partial = partial.transpose(3, 0, 2, 1, 4).reshape(shards, -1, LANES)
    with jax.named_scope("sum_features"):
        parts = exchange(partial, "fsdp").reshape(shards, 3, rows // halves, LANES)
        gate_value, up_value, back_hidden = jnp.sum(parts.astype(F32), axis=0)
    with jax.named_scope("activation"):
        sigmoid_gate = jax.nn.sigmoid(gate_value)
        activated = gate_value * sigmoid_gate
        hidden = (activated * up_value).astype(BF16)
        grad_gate_hidden = (
            back_hidden * up_value * sigmoid_gate * (1.0 + gate_value * (1.0 - sigmoid_gate))
        ).astype(BF16)
        grad_up_hidden = (back_hidden * activated).astype(BF16)
        shard = jnp.concatenate([grad_gate_hidden, grad_up_hidden, hidden], axis=0)
    with jax.named_scope("gather_hidden"):
        gathered = exchange(copies(shard, shards), "fsdp")
        gathered = gathered.reshape(padded // LANES, halves, 3, rows // halves, LANES)
        gathered = gathered.transpose(1, 3, 2, 0, 4).reshape(rows, 3 * padded)
    grad_in_hidden, hidden = gathered[:, : 2 * padded], gathered[:, 2 * padded :]

    with jax.named_scope("grad_rows"):
        in_slots = jnp.dot(order, grad_in_hidden, preferred_element_type=F32).astype(BF16)
        grad_rows = lax.dot_general(
            in_slots, w_in, (((1,), (1,)), ((), ())), preferred_element_type=F32
        )
        half = grad_rows.shape[0] // CORES
        grad_rows = grad_rows[:half] + lax.ppermute(
            grad_rows[half:], "dp", [(i, i ^ 1) for i in range(members)]
        )
        grad_rows = grad_rows.astype(BF16).reshape(members // CORES, -1, features)
        arrived = exchange(dense(grad_rows), "dp", CORE_GROUPS)
        grad_inputs = jnp.sum(arrived.astype(F32), axis=0, keepdims=True).astype(BF16)
        grad_inputs = undense(grad_inputs, grad_rows.shape[1])[0]

    contract_rows = (((0,), (0,)), ((), ()))
    with jax.named_scope("grad_weights"):
        in_total = lax.dot_general(
            kept_in, grad_in_hidden, contract_rows, preferred_element_type=F32
        )
        grad_in = (in_total * grad_scale).astype(BF16)
        down_total = lax.dot_general(hidden, kept_up, contract_rows, preferred_element_type=F32)
        grad_down = (down_total * grad_scale).astype(BF16)
    return (
        grad_inputs,
        grad_in[:, :hidden_units],
        grad_in[:, padded : padded + hidden_units],
        grad_down[:hidden_units],
    )


def solution(mesh):
    in_specs = (
        P("dp", "fsdp"),
        P("dp", "fsdp"),
        P("fsdp", "dp"),
        P("fsdp", "dp"),
        P("dp", "fsdp"),
        P(),
        P(),
    )
    out_specs = (P("dp", "fsdp"), P("fsdp", "dp"), P("fsdp", "dp"), P("dp", "fsdp"))
    return jax.shard_map(body, mesh=mesh, in_specs=in_specs, out_specs=out_specs, check_vma=False)
```

```python
import jax
import jax.numpy as jnp
from jax import lax
from jax.experimental import pallas as pl
from jax.experimental.pallas import tpu as pltpu
from jax.sharding import PartitionSpec as P

LANES = 128
CORES = 2
BF16 = jnp.bfloat16
F32 = jnp.float32
CORE_GROUPS = [[chip * CORES + core for chip in range(32)] for core in range(CORES)]


def exchange(x, axis, groups=None):
    return lax.all_to_all(x, axis, 0, 0, tiled=True, axis_index_groups=groups)


def copies(x, count):
    return jnp.broadcast_to(x[None], (count,) + x.shape)


def dense(x):
    n, rows, columns = x.shape
    tiles = columns // LANES
    return x.reshape(n, rows, tiles, LANES).transpose(0, 2, 1, 3).reshape(n, tiles * rows, LANES)


def undense(x, rows):
    n, flat, _ = x.shape
    tiles = flat // rows
    x = x.reshape(n, tiles, rows, LANES).transpose(0, 2, 1, 3)
    return x.reshape(n, rows, tiles * LANES)


def pad_hidden(weights):
    return jnp.pad(weights, ((0, -weights.shape[0] % (4 * LANES)), (0, 0)))


def call(kernel, outs, flops, *operands):
    whole = pl.BlockSpec(memory_space=pltpu.VMEM)
    moved = sum(x.size * x.dtype.itemsize for x in (*operands, *outs))
    return pl.pallas_call(
        kernel,
        out_shape=outs,
        in_specs=[whole] * len(operands),
        out_specs=[whole] * len(outs),
        cost_estimate=pl.CostEstimate(flops=flops, bytes_accessed=moved, transcendentals=0),
        compiler_params=pltpu.CompilerParams(vmem_limit_bytes=24 * 2**20),
    )(*operands)


def sums_kernel(mine_ref, other_ref, weights_ref, kept_ref, sums_ref):
    features = weights_ref.shape[1]
    padded = weights_ref.shape[0] // 3
    half = mine_ref.shape[0] // 2
    kept_ref[...] = mine_ref[...] + other_ref[...]
    step = 2 * LANES
    for which in range(3):
        first = 0 if which < 2 else features
        for at in range(0, padded, step):
            value = lax.dot_general(
                kept_ref[:, first : first + features],
                weights_ref[which * padded + at : which * padded + at + step, :],
                (((1,), (1,)), ((), ())),
                preferred_element_type=F32,
            ).astype(BF16)
            for tile in range(step // LANES):
                for part in range(2):
                    sums_ref[
                        2 * (at // LANES + tile) + part, which * half : (which + 1) * half, :
                    ] = value[part * half : (part + 1) * half, tile * LANES : (tile + 1) * LANES]


def rows_kernel(gathered_ref, weights_ref, order_ref, hidden_ref, rows_ref):
    shards, high, _ = gathered_ref.shape
    half = high // 3
    padded = shards // 2 * LANES
    for shard in range(shards):
        tile, part = divmod(shard, 2)
        for which in range(3):
            at = which * padded + tile * LANES
            hidden_ref[part * half : (part + 1) * half, at : at + LANES] = gathered_ref[
                shard, which * half : (which + 1) * half, :
            ]
    features = weights_ref.shape[1]
    for at in range(0, features, 2 * LANES):
        to = min(at + 2 * LANES, features)
        value = jnp.dot(
            hidden_ref[:, : 2 * padded],
            weights_ref[: 2 * padded, at:to],
            preferred_element_type=F32,
        ).astype(BF16)
        rows_ref[:, at:to] = jnp.dot(
            order_ref[...], value, preferred_element_type=F32
        ).astype(BF16)


def body(inputs, upstream, w_gate, w_up, w_down, lengths, move_dest):
    members = lax.axis_size("dp")
    shards = lax.axis_size("fsdp")
    core = lax.axis_index("dp") & 1
    capacity, features = inputs.shape
    hidden_units = w_gate.shape[1]
    heavy = members // 4
    rows = members * 4 + heavy * 2

    is_full = lengths == capacity
    full_rank = jnp.cumsum(is_full.astype(jnp.int32)) - is_full
    learner = jnp.arange(members, dtype=jnp.int32)[:, None]
    row = jnp.arange(capacity, dtype=jnp.int32)[None, :]
    target = jnp.repeat(move_dest, 2, axis=1)
    target = jnp.concatenate([jnp.zeros_like(target), target], axis=1)
    place = jnp.where(
        row < 2,
        learner * 4 + row,
        jnp.where(
            row < 4,
            members * 4 + full_rank[:, None] * 2 + row - 2,
            jnp.where(row < 6, learner * 4 + row - 2, target * 4 + 2 + row % 2),
        ),
    )
    place = jnp.where(row < lengths[:, None], place, -1)
    place = place.reshape(-1, CORES, capacity).transpose(1, 0, 2)
    place = jnp.where(core == 0, place[0], place[1]).reshape(-1)
    kept_row = jnp.arange(rows, dtype=jnp.int32)[None, :]
    pick = (kept_row.T == place[None, :]).astype(BF16)
    middle = jnp.where(is_full, members * 4 + full_rank * 2, -2)[:, None]
    pair = jnp.arange(2, dtype=jnp.int32)[None, :]
    none = jnp.full((members, 2), -1, jnp.int32)
    source = [learner * 4 + pair, middle + pair, learner * 4 + 2 + pair, none]
    source = jnp.concatenate(source, axis=1).reshape(-1)
    order = (source[:, None] == kept_row).astype(BF16)
    grad_scale = lax.rsqrt(jnp.sum(lengths).astype(F32))
    weights = jnp.concatenate([pad_hidden(w) for w in (w_gate.T, w_up.T, w_down)], axis=0)
    padded = weights.shape[0] // 3

    with jax.named_scope("gather_chips"):
        both = jnp.concatenate([inputs, upstream], axis=1)[None]
        got = exchange(copies(dense(both)[0], members // CORES), "dp", CORE_GROUPS)
        got, weights, order = lax.optimization_barrier((got, weights, order))
        got = undense(got, capacity).reshape(-1, 2 * features)
    with jax.named_scope("gather_core"):
        mine = jnp.dot(pick, got, preferred_element_type=F32).astype(BF16)
        other = lax.ppermute(mine, "dp", [(i, i ^ 1) for i in range(members)])
    with jax.named_scope("partial_sums"):
        kept, partial = call(
            sums_kernel,
            [
                jax.ShapeDtypeStruct(mine.shape, BF16),
                jax.ShapeDtypeStruct((shards, 3 * rows // 2, LANES), BF16),
            ],
            2 * rows * features * 3 * padded,
            mine,
            other,
            weights,
        )
    with jax.named_scope("sum_features"):
        parts = exchange(partial, "fsdp").reshape(shards, 3, rows // 2, LANES)
        gate_value, up_value, back_hidden = jnp.sum(parts.astype(F32), axis=0)
    with jax.named_scope("activation"):
        sigmoid_gate = jax.nn.sigmoid(gate_value)
        activated = gate_value * sigmoid_gate
        hidden = (activated * up_value).astype(BF16)
        grad_gate_hidden = (
            back_hidden * up_value * sigmoid_gate * (1.0 + gate_value * (1.0 - sigmoid_gate))
        ).astype(BF16)
        grad_up_hidden = (back_hidden * activated).astype(BF16)
        shard = jnp.concatenate([grad_gate_hidden, grad_up_hidden, hidden], axis=0)
    with jax.named_scope("gather_hidden"):
        gathered = exchange(copies(shard, shards), "fsdp")

    with jax.named_scope("grad_rows"):
        all_hidden, grad_rows = call(
            rows_kernel,
            [
                jax.ShapeDtypeStruct((rows, 3 * padded), BF16),
                jax.ShapeDtypeStruct((order.shape[0], features), BF16),
            ],
            2 * rows * features * (2 * padded + order.shape[0]),
            gathered,
            weights,
            order,
        )
        arrived = exchange(grad_rows.reshape(members, -1, features), "dp")
        grad_inputs = jnp.sum(arrived.astype(F32), axis=0)[: capacity // 2].astype(BF16)

    contract_rows = (((0,), (0,)), ((), ()))
    with jax.named_scope("grad_weights"):
        in_total = lax.dot_general(
            all_hidden[:, : 2 * padded],
            kept[:, :features],
            contract_rows,
            preferred_element_type=F32,
        )
        grad_in = (in_total * grad_scale).astype(BF16)
        down_total = lax.dot_general(
            all_hidden[:, 2 * padded :],
            kept[:, features:],
            contract_rows,
            preferred_element_type=F32,
        )
        grad_down = (down_total * grad_scale).astype(BF16)
    return (
        grad_inputs,
        grad_in[:hidden_units].T,
        grad_in[padded : padded + hidden_units].T,
        grad_down[:hidden_units],
    )


def solution(mesh):
    in_specs = (
        P("dp", "fsdp"),
        P("dp", "fsdp"),
        P("fsdp", "dp"),
        P("fsdp", "dp"),
        P("dp", "fsdp"),
        P(),
        P(),
    )
    out_specs = (P("dp", "fsdp"), P("fsdp", "dp"), P("fsdp", "dp"), P("dp", "fsdp"))
    return jax.shard_map(body, mesh=mesh, in_specs=in_specs, out_specs=out_specs, check_vma=False)
```

```python
import jax
import jax.numpy as jnp
from jax import lax
from jax.experimental import pallas as pl
from jax.experimental.pallas import tpu as pltpu
from jax.sharding import PartitionSpec as P

LANES = 128
CORES = 2
BF16 = jnp.bfloat16
F32 = jnp.float32
CORE_GROUPS = [[chip * CORES + core for chip in range(32)] for core in range(CORES)]


def exchange(x, axis, groups=None):
    return lax.all_to_all(x, axis, 0, 0, tiled=True, axis_index_groups=groups)


def copies(x, count):
    return jnp.broadcast_to(x[None], (count,) + x.shape)


def dense(x):
    n, rows, columns = x.shape
    tiles = columns // LANES
    return x.reshape(n, rows, tiles, LANES).transpose(0, 2, 1, 3).reshape(n, tiles * rows, LANES)


def undense(x, rows):
    n, flat, _ = x.shape
    tiles = flat // rows
    x = x.reshape(n, tiles, rows, LANES).transpose(0, 2, 1, 3)
    return x.reshape(n, rows, tiles * LANES)


def pad_hidden(weights):
    return jnp.pad(weights, ((0, -weights.shape[0] % (4 * LANES)), (0, 0)))


def call(kernel, outs, flops, *operands):
    whole = pl.BlockSpec(memory_space=pltpu.VMEM)
    moved = sum(x.size * x.dtype.itemsize for x in (*operands, *outs))
    return pl.pallas_call(
        kernel,
        out_shape=outs,
        in_specs=[whole] * len(operands),
        out_specs=[whole] * len(outs),
        cost_estimate=pl.CostEstimate(flops=flops, bytes_accessed=moved, transcendentals=0),
        compiler_params=pltpu.CompilerParams(vmem_limit_bytes=24 * 2**20),
    )(*operands)


def sums_kernel(mine_ref, other_ref, weights_ref, kept_ref, sums_ref):
    features = weights_ref.shape[1]
    padded = weights_ref.shape[0] // 3
    half = mine_ref.shape[0] // 2
    kept_ref[...] = mine_ref[...] + other_ref[...]
    step = 2 * LANES
    for which in range(3):
        first = 0 if which < 2 else features
        for at in range(0, padded, step):
            value = lax.dot_general(
                kept_ref[:, first : first + features],
                weights_ref[which * padded + at : which * padded + at + step, :],
                (((1,), (1,)), ((), ())),
                preferred_element_type=F32,
            ).astype(BF16)
            for tile in range(step // LANES):
                for part in range(2):
                    sums_ref[
                        2 * (at // LANES + tile) + part, which * half : (which + 1) * half, :
                    ] = value[part * half : (part + 1) * half, tile * LANES : (tile + 1) * LANES]


def rows_kernel(gathered_ref, weights_ref, hidden_ref, rows_ref):
    shards, high, _ = gathered_ref.shape
    half = high // 3
    padded = shards // 2 * LANES
    for shard in range(shards):
        tile, part = divmod(shard, 2)
        for which in range(3):
            at = which * padded + tile * LANES
            hidden_ref[part * half : (part + 1) * half, at : at + LANES] = gathered_ref[
                shard, which * half : (which + 1) * half, :
            ]
    features = weights_ref.shape[1]
    for at in range(0, features, 2 * LANES):
        to = min(at + 2 * LANES, features)
        rows_ref[:, at:to] = jnp.dot(
            hidden_ref[:, : 2 * padded],
            weights_ref[: 2 * padded, at:to],
            preferred_element_type=F32,
        ).astype(BF16)


def body(inputs, upstream, w_gate, w_up, w_down, lengths, move_dest):
    members = lax.axis_size("dp")
    shards = lax.axis_size("fsdp")
    core = lax.axis_index("dp") & 1
    capacity, features = inputs.shape
    hidden_units = w_gate.shape[1]
    heavy = members // 4
    rows = members * 4 + heavy * 2

    with jax.named_scope("gather_chips"):
        both = jnp.concatenate([inputs, upstream], axis=1)[None]
        got = exchange(copies(dense(both)[0], members // CORES), "dp", CORE_GROUPS)
        got, lengths, move_dest, w_gate, w_up, w_down = lax.optimization_barrier(
            (got, lengths, move_dest, w_gate, w_up, w_down)
        )
        theirs = lax.ppermute(got, "dp", [(i, i ^ 1) for i in range(members)])

    is_full = lengths == capacity
    full_rank = jnp.cumsum(is_full.astype(jnp.int32)) - is_full
    learner = jnp.arange(members, dtype=jnp.int32)[:, None]
    row = jnp.arange(capacity, dtype=jnp.int32)[None, :]
    target = jnp.repeat(move_dest, 2, axis=1)
    target = jnp.concatenate([jnp.zeros_like(target), target], axis=1)
    place = jnp.where(
        row < 2,
        learner * 4 + row,
        jnp.where(
            row < 4,
            members * 4 + full_rank[:, None] * 2 + row - 2,
            jnp.where(row < 6, learner * 4 + row - 2, target * 4 + 2 + row % 2),
        ),
    )
    place = jnp.where(row < lengths[:, None], place, -1)
    place = place.reshape(-1, CORES, capacity).transpose(1, 0, 2).reshape(CORES, -1)
    place = jnp.where(core == 0, place, place[::-1])
    kept_row = jnp.arange(rows, dtype=jnp.int32)
    pick = (kept_row[None, :, None] == place[:, None, :]).astype(BF16)
    full = jnp.where(is_full, full_rank, -1)
    spread = (full[:, None] == jnp.arange(heavy, dtype=jnp.int32)[None, :]).astype(BF16)
    grad_scale = lax.rsqrt(jnp.sum(lengths).astype(F32))
    weights = jnp.concatenate([pad_hidden(w) for w in (w_gate.T, w_up.T, w_down)], axis=0)
    padded = weights.shape[0] // 3

    with jax.named_scope("gather_core"):
        mine, other = [
            jnp.dot(
                pick[which],
                undense(part, capacity).reshape(-1, 2 * features),
                preferred_element_type=F32,
            ).astype(BF16)
            for which, part in enumerate((got, theirs))
        ]
    with jax.named_scope("partial_sums"):
        kept, partial = call(
            sums_kernel,
            [
                jax.ShapeDtypeStruct(mine.shape, BF16),
                jax.ShapeDtypeStruct((shards, 3 * rows // 2, LANES), BF16),
            ],
            2 * rows * features * 3 * padded,
            mine,
            other,
            weights,
        )
    with jax.named_scope("sum_features"):
        parts = exchange(partial, "fsdp").reshape(shards, 3, rows // 2, LANES)
        gate_value, up_value, back_hidden = jnp.sum(parts.astype(F32), axis=0)
    with jax.named_scope("activation"):
        sigmoid_gate = jax.nn.sigmoid(gate_value)
        activated = gate_value * sigmoid_gate
        hidden = (activated * up_value).astype(BF16)
        grad_gate_hidden = (
            back_hidden * up_value * sigmoid_gate * (1.0 + gate_value * (1.0 - sigmoid_gate))
        ).astype(BF16)
        grad_up_hidden = (back_hidden * activated).astype(BF16)
        shard = jnp.concatenate([grad_gate_hidden, grad_up_hidden, hidden], axis=0)
    with jax.named_scope("gather_hidden"):
        gathered = exchange(copies(shard, shards), "fsdp")

    with jax.named_scope("grad_rows"):
        all_hidden, grad_rows = call(
            rows_kernel,
            [
                jax.ShapeDtypeStruct((rows, 3 * padded), BF16),
                jax.ShapeDtypeStruct((rows, features), BF16),
            ],
            2 * rows * features * 2 * padded,
            gathered,
            weights,
        )
        outer = grad_rows[: members * 4].reshape(members, 2, 2, features)
        middle = jnp.einsum(
            "lh,htf->ltf",
            spread,
            grad_rows[members * 4 :].reshape(heavy, 2, features),
            preferred_element_type=F32,
        ).astype(BF16)
        slots = jnp.stack([outer[:, 0], middle, outer[:, 1]], axis=1).reshape(members, 6, features)
        message = jnp.pad(dense(slots), ((0, 0), (0, 2), (0, 0)))
        arrived = exchange(message, "dp")
        grad_inputs = jnp.sum(arrived.astype(F32), axis=0, keepdims=True)[:, :-2].astype(BF16)
        grad_inputs = undense(grad_inputs, 6)[0]

    contract_rows = (((0,), (0,)), ((), ()))
    with jax.named_scope("grad_weights"):
        in_total = lax.dot_general(
            all_hidden[:, : 2 * padded],
            kept[:, :features],
            contract_rows,
            preferred_element_type=F32,
        )
        grad_in = (in_total * grad_scale).astype(BF16)
        down_total = lax.dot_general(
            all_hidden[:, 2 * padded :],
            kept[:, features:],
            contract_rows,
            preferred_element_type=F32,
        )
        grad_down = (down_total * grad_scale).astype(BF16)
    return (
        grad_inputs,
        grad_in[:hidden_units].T,
        grad_in[padded : padded + hidden_units].T,
        grad_down[:hidden_units],
    )


def solution(mesh):
    in_specs = (
        P("dp", "fsdp"),
        P("dp", "fsdp"),
        P("fsdp", "dp"),
        P("fsdp", "dp"),
        P("dp", "fsdp"),
        P(),
        P(),
    )
    out_specs = (P("dp", "fsdp"), P("fsdp", "dp"), P("fsdp", "dp"), P("dp", "fsdp"))
    return jax.shard_map(body, mesh=mesh, in_specs=in_specs, out_specs=out_specs, check_vma=False)
```

```python
import jax
import jax.numpy as jnp
from jax import lax
from jax.experimental import pallas as pl
from jax.experimental.pallas import tpu as pltpu
from jax.sharding import PartitionSpec as P

LANES = 128
CORES = 2
BF16 = jnp.bfloat16
F32 = jnp.float32
CORE_GROUPS = [[chip * CORES + core for chip in range(32)] for core in range(CORES)]


def exchange(x, axis, groups=None):
    return lax.all_to_all(x, axis, 0, 0, tiled=True, axis_index_groups=groups)


def copies(x, count):
    return jnp.broadcast_to(x[None], (count,) + x.shape)


def dense(x):
    n, rows, columns = x.shape
    tiles = columns // LANES
    return x.reshape(n, rows, tiles, LANES).transpose(0, 2, 1, 3).reshape(n, tiles * rows, LANES)


def undense(x, rows):
    n, flat, _ = x.shape
    tiles = flat // rows
    x = x.reshape(n, tiles, rows, LANES).transpose(0, 2, 1, 3)
    return x.reshape(n, rows, tiles * LANES)


def pad_hidden(weights):
    return jnp.pad(weights, ((0, -weights.shape[0] % (4 * LANES)), (0, 0)))


def call(kernel, outs, flops, *operands, scratch=()):
    whole = pl.BlockSpec(memory_space=pltpu.VMEM)
    moved = sum(x.size * x.dtype.itemsize for x in (*operands, *outs))
    return pl.pallas_call(
        kernel,
        out_shape=outs,
        in_specs=[whole] * len(operands),
        out_specs=[whole] * len(outs),
        scratch_shapes=scratch,
        cost_estimate=pl.CostEstimate(flops=flops, bytes_accessed=moved, transcendentals=0),
        compiler_params=pltpu.CompilerParams(vmem_limit_bytes=24 * 2**20),
    )(*operands)


def sums_kernel(mine_ref, other_ref, weights_ref, kept_ref, sums_ref):
    features = weights_ref.shape[1]
    padded = weights_ref.shape[0] // 3
    half = mine_ref.shape[0] // 2
    kept_ref[...] = mine_ref[...] + other_ref[...]
    step = 2 * LANES
    for which in range(3):
        first = 0 if which < 2 else features
        for at in range(0, padded, step):
            value = lax.dot_general(
                kept_ref[:, first : first + features],
                weights_ref[which * padded + at : which * padded + at + step, :],
                (((1,), (1,)), ((), ())),
                preferred_element_type=F32,
            ).astype(BF16)
            for tile in range(step // LANES):
                for part in range(2):
                    sums_ref[
                        2 * (at // LANES + tile) + part, which * half : (which + 1) * half, :
                    ] = value[part * half : (part + 1) * half, tile * LANES : (tile + 1) * LANES]


def rows_kernel(gathered_ref, weights_ref, rows_ref, hidden_ref):
    shards, high, _ = gathered_ref.shape
    half = high // 3
    padded = shards // 2 * LANES
    for shard in range(shards):
        tile, part = divmod(shard, 2)
        for which in range(2):
            at = which * padded + tile * LANES
            hidden_ref[part * half : (part + 1) * half, at : at + LANES] = gathered_ref[
                shard, which * half : (which + 1) * half, :
            ]
    features = weights_ref.shape[1]
    for at in range(0, features, 2 * LANES):
        to = min(at + 2 * LANES, features)
        rows_ref[:, at:to] = jnp.dot(
            hidden_ref[...],
            weights_ref[: 2 * padded, at:to],
            preferred_element_type=F32,
        ).astype(BF16)


def body(inputs, upstream, w_gate, w_up, w_down, lengths, move_dest):
    members = lax.axis_size("dp")
    shards = lax.axis_size("fsdp")
    core = lax.axis_index("dp") & 1
    capacity, features = inputs.shape
    hidden_units = w_gate.shape[1]
    heavy = members // 4
    rows = members * 4 + heavy * 2

    is_full = lengths == capacity
    full_rank = jnp.cumsum(is_full.astype(jnp.int32)) - is_full
    learner = jnp.arange(members, dtype=jnp.int32)[:, None]
    row = jnp.arange(capacity, dtype=jnp.int32)[None, :]
    target = jnp.repeat(move_dest, 2, axis=1)
    target = jnp.concatenate([jnp.zeros_like(target), target], axis=1)
    place = jnp.where(
        row < 2,
        learner * 4 + row,
        jnp.where(
            row < 4,
            members * 4 + full_rank[:, None] * 2 + row - 2,
            jnp.where(row < 6, learner * 4 + row - 2, target * 4 + 2 + row % 2),
        ),
    )
    place = jnp.where(row < lengths[:, None], place, -1)
    place = place.reshape(-1, CORES, capacity).transpose(1, 0, 2)
    place = jnp.where(core == 0, place[0], place[1]).reshape(-1)
    pick = (jnp.arange(rows, dtype=jnp.int32)[:, None] == place[None, :]).astype(BF16)
    full = jnp.where(is_full, full_rank, -1)
    spread = (full[:, None] == jnp.arange(heavy, dtype=jnp.int32)[None, :]).astype(BF16)
    grad_scale = lax.rsqrt(jnp.sum(lengths).astype(F32))
    weights = jnp.concatenate([pad_hidden(w) for w in (w_gate.T, w_up.T, w_down)], axis=0)
    padded = weights.shape[0] // 3

    with jax.named_scope("gather_chips"):
        both = jnp.concatenate([inputs, upstream], axis=1)[None]
        got = exchange(copies(dense(both)[0], members // CORES), "dp", CORE_GROUPS)
        got, pick, weights, spread, grad_scale = lax.optimization_barrier(
            (got, pick, weights, spread, grad_scale)
        )
        got = undense(got, capacity).reshape(-1, 2 * features)
    with jax.named_scope("gather_core"):
        mine = jnp.dot(pick, got, preferred_element_type=F32).astype(BF16)
        other = lax.ppermute(mine, "dp", [(i, i ^ 1) for i in range(members)])
    with jax.named_scope("partial_sums"):
        kept, partial = call(
            sums_kernel,
            [
                jax.ShapeDtypeStruct(mine.shape, BF16),
                jax.ShapeDtypeStruct((shards, 3 * rows // 2, LANES), BF16),
            ],
            2 * rows * features * 3 * padded,
            mine,
            other,
            weights,
        )
    with jax.named_scope("sum_features"):
        parts = exchange(partial, "fsdp").reshape(shards, 3, rows // 2, LANES)
        gate_value, up_value, back_hidden = jnp.sum(parts.astype(F32), axis=0)
    with jax.named_scope("activation"):
        sigmoid_gate = jax.nn.sigmoid(gate_value)
        activated = gate_value * sigmoid_gate
        hidden = (activated * up_value).astype(BF16)
        grad_gate_hidden = (
            back_hidden * up_value * sigmoid_gate * (1.0 + gate_value * (1.0 - sigmoid_gate))
        ).astype(BF16)
        grad_up_hidden = (back_hidden * activated).astype(BF16)
        shard = jnp.concatenate([grad_gate_hidden, grad_up_hidden, hidden], axis=0)
    with jax.named_scope("gather_hidden"):
        gathered = exchange(copies(shard, shards), "fsdp")

    with jax.named_scope("grad_rows"):
        (grad_rows,) = call(
            rows_kernel,
            [jax.ShapeDtypeStruct((rows, features), BF16)],
            2 * rows * features * 2 * padded,
            gathered,
            weights,
            scratch=[pltpu.VMEM((rows, 2 * padded), BF16)],
        )
        outer = grad_rows[: members * 4].reshape(members, 2, 2, features)
        middle = jnp.einsum(
            "lh,htf->ltf",
            spread,
            grad_rows[members * 4 :].reshape(heavy, 2, features),
            preferred_element_type=F32,
        ).astype(BF16)
        slots = jnp.stack([outer[:, 0], middle, outer[:, 1]], axis=1).reshape(members, 6, features)
        arrived = exchange(dense(slots), "dp")
        grad_inputs = jnp.sum(arrived.astype(F32), axis=0, keepdims=True).astype(BF16)
        grad_inputs = undense(grad_inputs, 6)[0]

    contract_rows = (((0,), (0,)), ((), ()))
    with jax.named_scope("grad_weights"):
        all_hidden = gathered.reshape(padded // LANES, 2, 3, rows // 2, LANES)
        all_hidden = all_hidden.transpose(1, 3, 2, 0, 4).reshape(rows, 3 * padded)
        in_total = lax.dot_general(
            all_hidden[:, : 2 * padded],
            kept[:, :features],
            contract_rows,
            preferred_element_type=F32,
        )
        grad_in = (in_total * grad_scale).astype(BF16)
        down_total = lax.dot_general(
            all_hidden[:, 2 * padded :],
            kept[:, features:],
            contract_rows,
            preferred_element_type=F32,
        )
        grad_down = (down_total * grad_scale).astype(BF16)
    return (
        grad_inputs,
        grad_in[:hidden_units].T,
        grad_in[padded : padded + hidden_units].T,
        grad_down[:hidden_units],
    )


def solution(mesh):
    in_specs = (
        P("dp", "fsdp"),
        P("dp", "fsdp"),
        P("fsdp", "dp"),
        P("fsdp", "dp"),
        P("dp", "fsdp"),
        P(),
        P(),
    )
    out_specs = (P("dp", "fsdp"), P("fsdp", "dp"), P("fsdp", "dp"), P("dp", "fsdp"))
    return jax.shard_map(body, mesh=mesh, in_specs=in_specs, out_specs=out_specs, check_vma=False)
```

```python
import functools

import jax
import jax.numpy as jnp
from jax import lax
from jax.experimental import pallas as pl
from jax.experimental.pallas import tpu as pltpu
from jax.sharding import PartitionSpec as P

LANES = 128
CORES = 2
BF16 = jnp.bfloat16
F32 = jnp.float32
CORE_GROUPS = [[chip * CORES + core for chip in range(32)] for core in range(CORES)]


def exchange(x, axis, groups=None):
    return lax.all_to_all(x, axis, 0, 0, tiled=True, axis_index_groups=groups)


def copies(x, count):
    return jnp.broadcast_to(x[None], (count,) + x.shape)


def dense(x):
    n, rows, columns = x.shape
    tiles = columns // LANES
    return x.reshape(n, rows, tiles, LANES).transpose(0, 2, 1, 3).reshape(n, tiles * rows, LANES)


def undense(x, rows):
    n, flat, _ = x.shape
    tiles = flat // rows
    x = x.reshape(n, tiles, rows, LANES).transpose(0, 2, 1, 3)
    return x.reshape(n, rows, tiles * LANES)


def pad_hidden(weights):
    return jnp.pad(weights, ((0, -weights.shape[0] % (4 * LANES)), (0, 0)))


def call(kernel, outs, flops, *operands, scratch=()):
    whole = pl.BlockSpec(memory_space=pltpu.VMEM)
    scalars = pl.BlockSpec(memory_space=pltpu.SMEM)
    moved = sum(x.size * x.dtype.itemsize for x in (*operands, *outs))
    return pl.pallas_call(
        kernel,
        out_shape=outs,
        in_specs=[scalars if x.ndim == 1 else whole for x in operands],
        out_specs=[whole] * len(outs),
        scratch_shapes=scratch,
        cost_estimate=pl.CostEstimate(flops=flops, bytes_accessed=moved, transcendentals=0),
        compiler_params=pltpu.CompilerParams(vmem_limit_bytes=24 * 2**20),
    )(*operands)


def sums_kernel(mine_ref, other_ref, weights_ref, kept_ref, sums_ref):
    features = weights_ref.shape[1]
    padded = weights_ref.shape[0] // 3
    half = mine_ref.shape[0] // 2
    kept_ref[...] = mine_ref[...] + other_ref[...]
    step = 2 * LANES
    for which in range(3):
        first = 0 if which < 2 else features
        for at in range(0, padded, step):
            value = lax.dot_general(
                kept_ref[:, first : first + features],
                weights_ref[which * padded + at : which * padded + at + step, :],
                (((1,), (1,)), ((), ())),
                preferred_element_type=F32,
            ).astype(BF16)
            for tile in range(step // LANES):
                for part in range(2):
                    sums_ref[
                        2 * (at // LANES + tile) + part, which * half : (which + 1) * half, :
                    ] = value[part * half : (part + 1) * half, tile * LANES : (tile + 1) * LANES]


def rows_kernel(shared, core_ref, gathered_ref, weights_ref, own_ref, send_ref, hidden_ref, all_ref):
    shards, high, _ = gathered_ref.shape
    half = high // 3
    padded = shards // 2 * LANES
    for shard in range(shards):
        tile, part = divmod(shard, 2)
        for which in range(2):
            at = which * padded + tile * LANES
            hidden_ref[part * half : (part + 1) * half, at : at + LANES] = gathered_ref[
                shard, which * half : (which + 1) * half, :
            ]
    features = weights_ref.shape[1]
    for at in range(0, features, 2 * LANES):
        to = min(at + 2 * LANES, features)
        all_ref[:, at:to] = jnp.dot(
            hidden_ref[...],
            weights_ref[: 2 * padded, at:to],
            preferred_element_type=F32,
        )
    owned = (all_ref.shape[0] - shared) // CORES
    core = core_ref[0]
    for out_ref, which in ((own_ref, core), (send_ref, 1 - core)):
        out_ref[:owned, :] = all_ref[pl.ds(pl.multiple_of(which * owned, owned), owned), :]
        out_ref[owned:, :] = all_ref[CORES * owned :, :]


def body(inputs, upstream, w_gate, w_up, w_down, lengths, move_dest):
    members = lax.axis_size("dp")
    shards = lax.axis_size("fsdp")
    core = (lax.axis_index("dp") & 1).astype(jnp.int32)
    capacity, features = inputs.shape
    hidden_units = w_gate.shape[1]
    heavy = members // 4
    rows = members * 4 + heavy * 2

    is_full = lengths == capacity
    full_rank = jnp.cumsum(is_full.astype(jnp.int32)) - is_full
    learner = jnp.arange(members, dtype=jnp.int32)[:, None]
    row = jnp.arange(capacity, dtype=jnp.int32)[None, :]
    chips = members // CORES
    first = ((learner & 1) * chips + (learner >> 1)) * 4
    target = jnp.repeat(((move_dest & 1) * chips + (move_dest >> 1)) * 4, 2, axis=1)
    target = jnp.concatenate([jnp.zeros_like(target), target], axis=1)
    place = jnp.where(
        row < 2,
        first + row,
        jnp.where(
            row < 4,
            members * 4 + full_rank[:, None] * 2 + row - 2,
            jnp.where(row < 6, first + row - 2, target + 2 + row % 2),
        ),
    )
    place = jnp.where(row < lengths[:, None], place, -1)
    place = place.reshape(-1, CORES, capacity).transpose(1, 0, 2)
    place = jnp.where(core == 0, place[0], place[1]).reshape(-1)
    pick = (jnp.arange(rows, dtype=jnp.int32)[:, None] == place[None, :]).astype(BF16)
    full = jnp.where(is_full, full_rank, -1).reshape(-1, CORES)
    full = jnp.where(core == 0, full[:, 0], full[:, 1])
    spread = (full[:, None] == jnp.arange(heavy, dtype=jnp.int32)[None, :]).astype(BF16)
    grad_scale = lax.rsqrt(jnp.sum(lengths).astype(F32))
    weights = jnp.concatenate([pad_hidden(w) for w in (w_gate.T, w_up.T, w_down)], axis=0)
    padded = weights.shape[0] // 3

    with jax.named_scope("gather_chips"):
        both = jnp.concatenate([inputs, upstream], axis=1)[None]
        got = exchange(copies(dense(both)[0], members // CORES), "dp", CORE_GROUPS)
        got, pick, weights, spread, grad_scale = lax.optimization_barrier(
            (got, pick, weights, spread, grad_scale)
        )
        got = undense(got, capacity).reshape(-1, 2 * features)
    with jax.named_scope("gather_core"):
        mine = jnp.dot(pick, got, preferred_element_type=F32).astype(BF16)
        other = lax.ppermute(mine, "dp", [(i, i ^ 1) for i in range(members)])
    with jax.named_scope("partial_sums"):
        kept, partial = call(
            sums_kernel,
            [
                jax.ShapeDtypeStruct(mine.shape, BF16),
                jax.ShapeDtypeStruct((shards, 3 * rows // 2, LANES), BF16),
            ],
            2 * rows * features * 3 * padded,
            mine,
            other,
            weights,
        )
    with jax.named_scope("sum_features"):
        parts = exchange(partial, "fsdp").reshape(shards, 3, rows // 2, LANES)
        gate_value, up_value, back_hidden = jnp.sum(parts.astype(F32), axis=0)
    with jax.named_scope("activation"):
        sigmoid_gate = jax.nn.sigmoid(gate_value)
        activated = gate_value * sigmoid_gate
        hidden = (activated * up_value).astype(BF16)
        grad_gate_hidden = (
            back_hidden * up_value * sigmoid_gate * (1.0 + gate_value * (1.0 - sigmoid_gate))
        ).astype(BF16)
        grad_up_hidden = (back_hidden * activated).astype(BF16)
        shard = jnp.concatenate([grad_gate_hidden, grad_up_hidden, hidden], axis=0)
    with jax.named_scope("gather_hidden"):
        gathered = exchange(copies(shard, shards), "fsdp")

    with jax.named_scope("grad_rows"):
        own, send = call(
            functools.partial(rows_kernel, 2 * heavy),
            [jax.ShapeDtypeStruct((2 * members + 2 * heavy, features), F32)] * 2,
            2 * rows * features * 2 * padded,
            core[None],
            gathered,
            weights,
            scratch=[pltpu.VMEM((rows, 2 * padded), BF16), pltpu.VMEM((rows, features), F32)],
        )
        own, send, gathered = lax.optimization_barrier((own, send, gathered))
        grad_rows = own + lax.ppermute(send, "dp", [(i, i ^ 1) for i in range(members)])
        grad_rows = grad_rows.astype(BF16)
        outer = grad_rows[: 2 * members].reshape(chips, 2, 2, features)
        middle = jnp.einsum(
            "lh,htf->ltf",
            spread,
            grad_rows[2 * members :].reshape(heavy, 2, features),
            preferred_element_type=F32,
        ).astype(BF16)
        slots = jnp.stack([outer[:, 0], middle, outer[:, 1]], axis=1).reshape(chips, 6, features)
        arrived = exchange(dense(slots), "dp", CORE_GROUPS)
        grad_inputs = jnp.sum(arrived.astype(F32), axis=0, keepdims=True).astype(BF16)
        grad_inputs = undense(grad_inputs, 6)[0]

    contract_rows = (((0,), (0,)), ((), ()))
    with jax.named_scope("grad_weights"):
        all_hidden = gathered.reshape(padded // LANES, 2, 3, rows // 2, LANES)
        all_hidden = all_hidden.transpose(1, 3, 2, 0, 4).reshape(rows, 3 * padded)
        in_total = lax.dot_general(
            all_hidden[:, : 2 * padded],
            kept[:, :features],
            contract_rows,
            preferred_element_type=F32,
        )
        grad_in = (in_total * grad_scale).astype(BF16)
        down_total = lax.dot_general(
            all_hidden[:, 2 * padded :],
            kept[:, features:],
            contract_rows,
            preferred_element_type=F32,
        )
        grad_down = (down_total * grad_scale).astype(BF16)
    return (
        grad_inputs,
        grad_in[:hidden_units].T,
        grad_in[padded : padded + hidden_units].T,
        grad_down[:hidden_units],
    )


def solution(mesh):
    in_specs = (
        P("dp", "fsdp"),
        P("dp", "fsdp"),
        P("fsdp", "dp"),
        P("fsdp", "dp"),
        P("dp", "fsdp"),
        P(),
        P(),
    )
    out_specs = (P("dp", "fsdp"), P("fsdp", "dp"), P("fsdp", "dp"), P("dp", "fsdp"))
    return jax.shard_map(body, mesh=mesh, in_specs=in_specs, out_specs=out_specs, check_vma=False)
```

```python
import functools

import jax
import jax.numpy as jnp
from jax import lax
from jax.experimental import pallas as pl
from jax.experimental.pallas import tpu as pltpu
from jax.sharding import PartitionSpec as P

LANES = 128
CORES = 2
BF16 = jnp.bfloat16
F32 = jnp.float32
CORE_GROUPS = [[chip * CORES + core for chip in range(32)] for core in range(CORES)]


def exchange(x, axis, groups=None):
    return lax.all_to_all(x, axis, 0, 0, tiled=True, axis_index_groups=groups)


def copies(x, count):
    return jnp.broadcast_to(x[None], (count,) + x.shape)


def dense(x):
    n, rows, columns = x.shape
    tiles = columns // LANES
    return x.reshape(n, rows, tiles, LANES).transpose(0, 2, 1, 3).reshape(n, tiles * rows, LANES)


def undense(x, rows):
    n, flat, _ = x.shape
    tiles = flat // rows
    x = x.reshape(n, tiles, rows, LANES).transpose(0, 2, 1, 3)
    return x.reshape(n, rows, tiles * LANES)


def pad_hidden(weights):
    return jnp.pad(weights, ((0, -weights.shape[0] % (4 * LANES)), (0, 0)))


def call(kernel, outs, flops, *operands, scratch=()):
    whole = pl.BlockSpec(memory_space=pltpu.VMEM)
    scalars = pl.BlockSpec(memory_space=pltpu.SMEM)
    moved = sum(x.size * x.dtype.itemsize for x in (*operands, *outs))
    return pl.pallas_call(
        kernel,
        out_shape=outs,
        in_specs=[scalars if x.ndim == 1 else whole for x in operands],
        out_specs=[whole] * len(outs),
        scratch_shapes=scratch,
        cost_estimate=pl.CostEstimate(flops=flops, bytes_accessed=moved, transcendentals=0),
        compiler_params=pltpu.CompilerParams(vmem_limit_bytes=24 * 2**20),
    )(*operands)


def sums_kernel(mine_ref, other_ref, weights_ref, kept_ref, sums_ref):
    features = weights_ref.shape[1]
    padded = weights_ref.shape[0] // 3
    half = mine_ref.shape[0] // 2
    kept_ref[...] = mine_ref[...] + other_ref[...]
    step = 2 * LANES
    for which in range(3):
        first = 0 if which < 2 else features
        for at in range(0, padded, step):
            value = lax.dot_general(
                kept_ref[:, first : first + features],
                weights_ref[which * padded + at : which * padded + at + step, :],
                (((1,), (1,)), ((), ())),
                preferred_element_type=F32,
            ).astype(BF16)
            for tile in range(step // LANES):
                for part in range(2):
                    sums_ref[
                        2 * (at // LANES + tile) + part, which * half : (which + 1) * half, :
                    ] = value[part * half : (part + 1) * half, tile * LANES : (tile + 1) * LANES]


def rows_kernel(shared, core_ref, gathered_ref, weights_ref, own_ref, send_ref, hidden_ref, all_ref):
    shards, high, _ = gathered_ref.shape
    half = high // 3
    padded = shards // 2 * LANES
    for shard in range(shards):
        tile, part = divmod(shard, 2)
        for which in range(2):
            at = which * padded + tile * LANES
            hidden_ref[part * half : (part + 1) * half, at : at + LANES] = gathered_ref[
                shard, which * half : (which + 1) * half, :
            ]
    features = weights_ref.shape[1]
    for at in range(0, features, 2 * LANES):
        to = min(at + 2 * LANES, features)
        all_ref[:, at:to] = jnp.dot(
            hidden_ref[...],
            weights_ref[: 2 * padded, at:to],
            preferred_element_type=F32,
        )
    owned = (all_ref.shape[0] - shared) // CORES
    core = core_ref[0]
    for out_ref, which in ((own_ref, core), (send_ref, 1 - core)):
        out_ref[:owned, :] = all_ref[pl.ds(pl.multiple_of(which * owned, owned), owned), :]
        out_ref[owned:, :] = all_ref[CORES * owned :, :]


def body(inputs, upstream, w_gate, w_up, w_down, lengths, move_dest):
    members = lax.axis_size("dp")
    shards = lax.axis_size("fsdp")
    core = (lax.axis_index("dp") & 1).astype(jnp.int32)
    capacity, features = inputs.shape
    hidden_units = w_gate.shape[1]
    heavy = members // 4
    rows = members * 4 + heavy * 2

    is_full = lengths == capacity
    full_rank = jnp.cumsum(is_full.astype(jnp.int32)) - is_full
    learner = jnp.arange(members, dtype=jnp.int32)[:, None]
    row = jnp.arange(capacity, dtype=jnp.int32)[None, :]
    chips = members // CORES
    first = ((learner & 1) * chips + (learner >> 1)) * 4
    target = jnp.repeat(((move_dest & 1) * chips + (move_dest >> 1)) * 4, 2, axis=1)
    target = jnp.concatenate([jnp.zeros_like(target), target], axis=1)
    place = jnp.where(
        row < 2,
        first + row,
        jnp.where(
            row < 4,
            members * 4 + full_rank[:, None] * 2 + row - 2,
            jnp.where(row < 6, first + row - 2, target + 2 + row % 2),
        ),
    )
    place = jnp.where(row < lengths[:, None], place, -1)
    place = place.reshape(-1, CORES, capacity).transpose(1, 0, 2)
    place = jnp.where(core == 0, place[0], place[1]).reshape(-1)
    pick = (jnp.arange(rows, dtype=jnp.int32)[:, None] == place[None, :]).astype(BF16)
    full = jnp.where(is_full, full_rank, -1).reshape(-1, CORES)
    full = jnp.where(core == 0, full[:, 0], full[:, 1])
    spread = (full[:, None] == jnp.arange(heavy, dtype=jnp.int32)[None, :]).astype(BF16)
    grad_scale = lax.rsqrt(jnp.sum(lengths).astype(F32))
    weights = jnp.concatenate([pad_hidden(w) for w in (w_gate.T, w_up.T, w_down)], axis=0)
    padded = weights.shape[0] // 3

    with jax.named_scope("gather_chips"):
        both = jnp.concatenate([inputs, upstream], axis=1)[None]
        got = exchange(copies(dense(both)[0], members // CORES), "dp", CORE_GROUPS)
        got, pick, weights, spread, grad_scale = lax.optimization_barrier(
            (got, pick, weights, spread, grad_scale)
        )
        got = undense(got, capacity).reshape(-1, 2 * features)
    with jax.named_scope("gather_core"):
        mine = jnp.dot(pick, got, preferred_element_type=F32).astype(BF16)
        other = lax.ppermute(mine, "dp", [(i, i ^ 1) for i in range(members)])
    with jax.named_scope("partial_sums"):
        kept, partial = call(
            sums_kernel,
            [
                jax.ShapeDtypeStruct(mine.shape, BF16),
                jax.ShapeDtypeStruct((shards, 3 * rows // 2, LANES), BF16),
            ],
            2 * rows * features * 3 * padded,
            mine,
            other,
            weights,
        )
    with jax.named_scope("sum_features"):
        parts = exchange(partial, "fsdp").reshape(shards, 3, rows // 2, LANES)
        gate_value, up_value, back_hidden = jnp.sum(parts.astype(F32), axis=0)
    with jax.named_scope("activation"):
        sigmoid_gate = jax.nn.sigmoid(gate_value)
        activated = gate_value * sigmoid_gate
        hidden = (activated * up_value).astype(BF16)
        grad_gate_hidden = (
            back_hidden * up_value * sigmoid_gate * (1.0 + gate_value * (1.0 - sigmoid_gate))
        ).astype(BF16)
        grad_up_hidden = (back_hidden * activated).astype(BF16)
        shard = jnp.concatenate([grad_gate_hidden, grad_up_hidden, hidden], axis=0)
    with jax.named_scope("gather_hidden"):
        gathered = exchange(copies(shard, shards), "fsdp")

    with jax.named_scope("grad_rows"):
        own, send = call(
            functools.partial(rows_kernel, 2 * heavy),
            [jax.ShapeDtypeStruct((2 * members + 2 * heavy, features), F32)] * 2,
            2 * rows * features * 2 * padded,
            core[None],
            gathered,
            weights,
            scratch=[pltpu.VMEM((rows, 2 * padded), BF16), pltpu.VMEM((rows, features), F32)],
        )
        own, send, gathered = lax.optimization_barrier((own, send, gathered))
        grad_rows = own + lax.ppermute(send, "dp", [(i, i ^ 1) for i in range(members)])
        all_hidden = gathered.reshape(padded // LANES, 2, 3, rows // 2, LANES)
        all_hidden = all_hidden.transpose(1, 3, 2, 0, 4).reshape(rows, 3 * padded)
        grad_rows = grad_rows.astype(BF16)
        outer = grad_rows[: 2 * members].reshape(chips, 2, 2, features)
        middle = jnp.einsum(
            "lh,htf->ltf",
            spread,
            grad_rows[2 * members :].reshape(heavy, 2, features),
            preferred_element_type=F32,
        ).astype(BF16)
        slots = jnp.stack([outer[:, 0], middle, outer[:, 1]], axis=1).reshape(chips, 6, features)
        message, all_hidden, kept = lax.optimization_barrier((dense(slots), all_hidden, kept))
        arrived = exchange(message, "dp", CORE_GROUPS)
        grad_inputs = jnp.sum(arrived.astype(F32), axis=0, keepdims=True).astype(BF16)
        grad_inputs = undense(grad_inputs, 6)[0]

    contract_rows = (((0,), (0,)), ((), ()))
    with jax.named_scope("grad_weights"):
        in_total = lax.dot_general(
            all_hidden[:, : 2 * padded],
            kept[:, :features],
            contract_rows,
            preferred_element_type=F32,
        )
        grad_in = (in_total * grad_scale).astype(BF16)
        down_total = lax.dot_general(
            all_hidden[:, 2 * padded :],
            kept[:, features:],
            contract_rows,
            preferred_element_type=F32,
        )
        grad_down = (down_total * grad_scale).astype(BF16)
    return (
        grad_inputs,
        grad_in[:hidden_units].T,
        grad_in[padded : padded + hidden_units].T,
        grad_down[:hidden_units],
    )


def solution(mesh):
    in_specs = (
        P("dp", "fsdp"),
        P("dp", "fsdp"),
        P("fsdp", "dp"),
        P("fsdp", "dp"),
        P("dp", "fsdp"),
        P(),
        P(),
    )
    out_specs = (P("dp", "fsdp"), P("fsdp", "dp"), P("fsdp", "dp"), P("dp", "fsdp"))
    return jax.shard_map(body, mesh=mesh, in_specs=in_specs, out_specs=out_specs, check_vma=False)
```

```python
import functools

import jax
import jax.numpy as jnp
from jax import lax
from jax.experimental import pallas as pl
from jax.experimental.pallas import tpu as pltpu
from jax.sharding import PartitionSpec as P

LANES = 128
CORES = 2
BF16 = jnp.bfloat16
F32 = jnp.float32
Y_CHIPS = 8
Z_CHIPS = 4
CORE_GROUPS = [[chip * CORES + core for chip in range(32)] for core in range(CORES)]


def dp_index(z, y, core):
    return (z * Y_CHIPS + y) * CORES + core


Z_GROUPS = [
    [dp_index(z, y, core) for z in range(Z_CHIPS)]
    for y in range(Y_CHIPS)
    for core in range(CORES)
]
Y_GROUPS = [
    [dp_index(z, y, core) for y in range(Y_CHIPS)]
    for z in range(Z_CHIPS)
    for core in range(CORES)
]


def exchange(x, axis, groups=None):
    return lax.all_to_all(x, axis, 0, 0, tiled=True, axis_index_groups=groups)


def copies(x, count):
    return jnp.broadcast_to(x[None], (count,) + x.shape)


def dense(x):
    n, rows, columns = x.shape
    tiles = columns // LANES
    return x.reshape(n, rows, tiles, LANES).transpose(0, 2, 1, 3).reshape(n, tiles * rows, LANES)


def undense(x, rows):
    n, flat, _ = x.shape
    tiles = flat // rows
    x = x.reshape(n, tiles, rows, LANES).transpose(0, 2, 1, 3)
    return x.reshape(n, rows, tiles * LANES)


def pad_hidden(weights):
    return jnp.pad(weights, ((0, -weights.shape[0] % (4 * LANES)), (0, 0)))


def call(kernel, outs, flops, *operands, scratch=()):
    whole = pl.BlockSpec(memory_space=pltpu.VMEM)
    scalars = pl.BlockSpec(memory_space=pltpu.SMEM)
    moved = sum(x.size * x.dtype.itemsize for x in (*operands, *outs))
    return pl.pallas_call(
        kernel,
        out_shape=outs,
        in_specs=[scalars if x.ndim == 1 else whole for x in operands],
        out_specs=[whole] * len(outs),
        scratch_shapes=scratch,
        cost_estimate=pl.CostEstimate(flops=flops, bytes_accessed=moved, transcendentals=0),
        compiler_params=pltpu.CompilerParams(vmem_limit_bytes=24 * 2**20),
    )(*operands)


def sums_kernel(mine_ref, other_ref, weights_ref, kept_ref, sums_ref):
    features = weights_ref.shape[1]
    padded = weights_ref.shape[0] // 3
    half = mine_ref.shape[0] // 2
    kept_ref[...] = mine_ref[...] + other_ref[...]
    step = 2 * LANES
    for which in range(3):
        first = 0 if which < 2 else features
        for at in range(0, padded, step):
            value = lax.dot_general(
                kept_ref[:, first : first + features],
                weights_ref[which * padded + at : which * padded + at + step, :],
                (((1,), (1,)), ((), ())),
                preferred_element_type=F32,
            ).astype(BF16)
            for tile in range(step // LANES):
                for part in range(2):
                    sums_ref[
                        2 * (at // LANES + tile) + part, which * half : (which + 1) * half, :
                    ] = value[part * half : (part + 1) * half, tile * LANES : (tile + 1) * LANES]


def rows_kernel(shared, core_ref, gathered_ref, weights_ref, own_ref, send_ref, hidden_ref, all_ref):
    shards, high, _ = gathered_ref.shape
    half = high // 3
    padded = shards // 2 * LANES
    for shard in range(shards):
        tile, part = divmod(shard, 2)
        for which in range(2):
            at = which * padded + tile * LANES
            hidden_ref[part * half : (part + 1) * half, at : at + LANES] = gathered_ref[
                shard, which * half : (which + 1) * half, :
            ]
    features = weights_ref.shape[1]
    for at in range(0, features, 2 * LANES):
        to = min(at + 2 * LANES, features)
        all_ref[:, at:to] = jnp.dot(
            hidden_ref[...],
            weights_ref[: 2 * padded, at:to],
            preferred_element_type=F32,
        )
    owned = (all_ref.shape[0] - shared) // CORES
    core = core_ref[0]
    for out_ref, which in ((own_ref, core), (send_ref, 1 - core)):
        out_ref[:owned, :] = all_ref[pl.ds(pl.multiple_of(which * owned, owned), owned), :]
        out_ref[owned:, :] = all_ref[CORES * owned :, :]


def body(inputs, upstream, w_gate, w_up, w_down, lengths, move_dest):
    members = lax.axis_size("dp")
    shards = lax.axis_size("fsdp")
    core = (lax.axis_index("dp") & 1).astype(jnp.int32)
    capacity, features = inputs.shape
    hidden_units = w_gate.shape[1]
    heavy = members // 4
    rows = members * 4 + heavy * 2

    is_full = lengths == capacity
    full_rank = jnp.cumsum(is_full.astype(jnp.int32)) - is_full
    learner = jnp.arange(members, dtype=jnp.int32)[:, None]
    row = jnp.arange(capacity, dtype=jnp.int32)[None, :]
    chips = members // CORES
    first = ((learner & 1) * chips + (learner >> 1)) * 4
    target = jnp.repeat(((move_dest & 1) * chips + (move_dest >> 1)) * 4, 2, axis=1)
    target = jnp.concatenate([jnp.zeros_like(target), target], axis=1)
    place = jnp.where(
        row < 2,
        first + row,
        jnp.where(
            row < 4,
            members * 4 + full_rank[:, None] * 2 + row - 2,
            jnp.where(row < 6, first + row - 2, target + 2 + row % 2),
        ),
    )
    place = jnp.where(row < lengths[:, None], place, -1)
    place = place.reshape(Z_CHIPS, Y_CHIPS, CORES, capacity).transpose(2, 1, 0, 3)
    place = jnp.where(core == 0, place[0], place[1]).reshape(-1)
    pick = (jnp.arange(rows, dtype=jnp.int32)[:, None] == place[None, :]).astype(BF16)
    full = jnp.where(is_full, full_rank, -1).reshape(-1, CORES)
    full = jnp.where(core == 0, full[:, 0], full[:, 1])
    spread = (full[:, None] == jnp.arange(heavy, dtype=jnp.int32)[None, :]).astype(BF16)
    grad_scale = lax.rsqrt(jnp.sum(lengths).astype(F32))
    weights = jnp.concatenate([pad_hidden(w) for w in (w_gate.T, w_up.T, w_down)], axis=0)
    padded = weights.shape[0] // 3

    with jax.named_scope("gather_chips"):
        both = jnp.concatenate([inputs, upstream], axis=1)[None]
        got = exchange(copies(dense(both)[0], Z_CHIPS), "dp", Z_GROUPS)
        got = undense(got, capacity).reshape(1, Z_CHIPS * capacity, 2 * features)
        got = dense(got)[0]
        got, pick, weights, spread, grad_scale = lax.optimization_barrier(
            (got, pick, weights, spread, grad_scale)
        )
        got = exchange(copies(got, Y_CHIPS), "dp", Y_GROUPS)
        got = undense(got, Z_CHIPS * capacity).reshape(-1, 2 * features)
    with jax.named_scope("gather_core"):
        mine = jnp.dot(pick, got, preferred_element_type=F32).astype(BF16)
        other = lax.ppermute(mine, "dp", [(i, i ^ 1) for i in range(members)])
    with jax.named_scope("partial_sums"):
        kept, partial = call(
            sums_kernel,
            [
                jax.ShapeDtypeStruct(mine.shape, BF16),
                jax.ShapeDtypeStruct((shards, 3 * rows // 2, LANES), BF16),
            ],
            2 * rows * features * 3 * padded,
            mine,
            other,
            weights,
        )
    with jax.named_scope("sum_features"):
        parts = exchange(partial, "fsdp").reshape(shards, 3, rows // 2, LANES)
        gate_value, up_value, back_hidden = jnp.sum(parts.astype(F32), axis=0)
    with jax.named_scope("activation"):
        sigmoid_gate = jax.nn.sigmoid(gate_value)
        activated = gate_value * sigmoid_gate
        hidden = (activated * up_value).astype(BF16)
        grad_gate_hidden = (
            back_hidden * up_value * sigmoid_gate * (1.0 + gate_value * (1.0 - sigmoid_gate))
        ).astype(BF16)
        grad_up_hidden = (back_hidden * activated).astype(BF16)
        shard = jnp.concatenate([grad_gate_hidden, grad_up_hidden, hidden], axis=0)
    with jax.named_scope("gather_hidden"):
        gathered = exchange(copies(shard, shards), "fsdp")

    with jax.named_scope("grad_rows"):
        own, send = call(
            functools.partial(rows_kernel, 2 * heavy),
            [jax.ShapeDtypeStruct((2 * members + 2 * heavy, features), F32)] * 2,
            2 * rows * features * 2 * padded,
            core[None],
            gathered,
            weights,
            scratch=[pltpu.VMEM((rows, 2 * padded), BF16), pltpu.VMEM((rows, features), F32)],
        )
        own, send, gathered = lax.optimization_barrier((own, send, gathered))
        grad_rows = own + lax.ppermute(send, "dp", [(i, i ^ 1) for i in range(members)])
        all_hidden = gathered.reshape(padded // LANES, 2, 3, rows // 2, LANES)
        all_hidden = all_hidden.transpose(1, 3, 2, 0, 4).reshape(rows, 3 * padded)
        grad_rows = grad_rows.astype(BF16)
        outer = grad_rows[: 2 * members].reshape(chips, 2, 2, features)
        middle = jnp.einsum(
            "lh,htf->ltf",
            spread,
            grad_rows[2 * members :].reshape(heavy, 2, features),
            preferred_element_type=F32,
        ).astype(BF16)
        slots = jnp.stack([outer[:, 0], middle, outer[:, 1]], axis=1).reshape(chips, 6, features)
        message, all_hidden, kept = lax.optimization_barrier((dense(slots), all_hidden, kept))
        arrived = exchange(message, "dp", CORE_GROUPS)
        grad_inputs = jnp.sum(arrived.astype(F32), axis=0, keepdims=True).astype(BF16)
        grad_inputs = undense(grad_inputs, 6)[0]

    contract_rows = (((0,), (0,)), ((), ()))
    with jax.named_scope("grad_weights"):
        in_total = lax.dot_general(
            all_hidden[:, : 2 * padded],
            kept[:, :features],
            contract_rows,
            preferred_element_type=F32,
        )
        grad_in = (in_total * grad_scale).astype(BF16)
        down_total = lax.dot_general(
            all_hidden[:, 2 * padded :],
            kept[:, features:],
            contract_rows,
            preferred_element_type=F32,
        )
        grad_down = (down_total * grad_scale).astype(BF16)
    return (
        grad_inputs,
        grad_in[:hidden_units].T,
        grad_in[padded : padded + hidden_units].T,
        grad_down[:hidden_units],
    )


def solution(mesh):
    in_specs = (
        P("dp", "fsdp"),
        P("dp", "fsdp"),
        P("fsdp", "dp"),
        P("fsdp", "dp"),
        P("dp", "fsdp"),
        P(),
        P(),
    )
    out_specs = (P("dp", "fsdp"), P("fsdp", "dp"), P("fsdp", "dp"), P("dp", "fsdp"))
    return jax.shard_map(body, mesh=mesh, in_specs=in_specs, out_specs=out_specs, check_vma=False)
```

```python
import functools

import jax
import jax.numpy as jnp
from jax import lax
from jax.experimental import pallas as pl
from jax.experimental.pallas import tpu as pltpu
from jax.sharding import PartitionSpec as P

LANES = 128
CORES = 2
BF16 = jnp.bfloat16
F32 = jnp.float32
CORE_GROUPS = [[chip * CORES + core for chip in range(32)] for core in range(CORES)]


def exchange(x, axis, groups=None):
    return lax.all_to_all(x, axis, 0, 0, tiled=True, axis_index_groups=groups)


def copies(x, count):
    return jnp.broadcast_to(x[None], (count,) + x.shape)


def dense(x):
    n, rows, columns = x.shape
    tiles = columns // LANES
    return x.reshape(n, rows, tiles, LANES).transpose(0, 2, 1, 3).reshape(n, tiles * rows, LANES)


def undense(x, rows):
    n, flat, _ = x.shape
    tiles = flat // rows
    x = x.reshape(n, tiles, rows, LANES).transpose(0, 2, 1, 3)
    return x.reshape(n, rows, tiles * LANES)


def pad_hidden(weights):
    return jnp.pad(weights, ((0, -weights.shape[0] % (4 * LANES)), (0, 0)))


def call(kernel, outs, flops, *operands, scratch=()):
    whole = pl.BlockSpec(memory_space=pltpu.VMEM)
    scalars = pl.BlockSpec(memory_space=pltpu.SMEM)
    moved = sum(x.size * x.dtype.itemsize for x in (*operands, *outs))
    return pl.pallas_call(
        kernel,
        out_shape=outs,
        in_specs=[scalars if x.ndim == 1 else whole for x in operands],
        out_specs=[whole] * len(outs),
        scratch_shapes=scratch,
        cost_estimate=pl.CostEstimate(flops=flops, bytes_accessed=moved, transcendentals=0),
        compiler_params=pltpu.CompilerParams(vmem_limit_bytes=24 * 2**20),
    )(*operands)


def sums_kernel(mine_ref, other_ref, weights_ref, kept_ref, sums_ref):
    features = weights_ref.shape[1]
    padded = weights_ref.shape[0] // 3
    half = mine_ref.shape[0] // 2
    kept_ref[...] = mine_ref[...] + other_ref[...]
    step = 2 * LANES
    for which in range(3):
        first = 0 if which < 2 else features
        for at in range(0, padded, step):
            value = lax.dot_general(
                kept_ref[:, first : first + features],
                weights_ref[which * padded + at : which * padded + at + step, :],
                (((1,), (1,)), ((), ())),
                preferred_element_type=F32,
            ).astype(BF16)
            for tile in range(step // LANES):
                for part in range(2):
                    sums_ref[
                        2 * (at // LANES + tile) + part, which * half : (which + 1) * half, :
                    ] = value[part * half : (part + 1) * half, tile * LANES : (tile + 1) * LANES]


def rows_kernel(shared, core_ref, gathered_ref, weights_ref, own_ref, send_ref, hidden_ref, all_ref):
    shards, high, _ = gathered_ref.shape
    half = high // 3
    padded = shards // 2 * LANES
    for shard in range(shards):
        tile, part = divmod(shard, 2)
        for which in range(2):
            at = which * padded + tile * LANES
            hidden_ref[part * half : (part + 1) * half, at : at + LANES] = gathered_ref[
                shard, which * half : (which + 1) * half, :
            ]
    features = weights_ref.shape[1]
    for at in range(0, features, 2 * LANES):
        to = min(at + 2 * LANES, features)
        all_ref[:, at:to] = jnp.dot(
            hidden_ref[...],
            weights_ref[: 2 * padded, at:to],
            preferred_element_type=F32,
        )
    owned = (all_ref.shape[0] - shared) // CORES
    core = core_ref[0]
    for out_ref, which in ((own_ref, core), (send_ref, 1 - core)):
        out_ref[:owned, :] = all_ref[pl.ds(pl.multiple_of(which * owned, owned), owned), :]
        out_ref[owned:, :] = all_ref[CORES * owned :, :]


def body(inputs, upstream, w_gate, w_up, w_down, lengths, move_dest):
    members = lax.axis_size("dp")
    shards = lax.axis_size("fsdp")
    core = (lax.axis_index("dp") & 1).astype(jnp.int32)
    capacity, features = inputs.shape
    hidden_units = w_gate.shape[1]
    heavy = members // 4
    rows = members * 4 + heavy * 2

    is_full = lengths == capacity
    full_rank = jnp.cumsum(is_full.astype(jnp.int32)) - is_full
    learner = jnp.arange(members, dtype=jnp.int32)[:, None]
    row = jnp.arange(capacity, dtype=jnp.int32)[None, :]
    chips = members // CORES
    first = ((learner & 1) * chips + (learner >> 1)) * 4
    target = jnp.repeat(((move_dest & 1) * chips + (move_dest >> 1)) * 4, 2, axis=1)
    target = jnp.concatenate([jnp.zeros_like(target), target], axis=1)
    place = jnp.where(
        row < 2,
        first + row,
        jnp.where(
            row < 4,
            members * 4 + full_rank[:, None] * 2 + row - 2,
            jnp.where(row < 6, first + row - 2, target + 2 + row % 2),
        ),
    )
    place = jnp.where(row < lengths[:, None], place, -1)
    place = place.reshape(-1, CORES, capacity).transpose(1, 0, 2)
    place = jnp.where(core == 0, place[0], place[1]).reshape(-1)
    pick = (jnp.arange(rows, dtype=jnp.int32)[:, None] == place[None, :]).astype(BF16)
    full = jnp.where(is_full, full_rank, -1).reshape(-1, CORES)
    full = jnp.where(core == 0, full[:, 0], full[:, 1])
    spread = (full[:, None] == jnp.arange(heavy, dtype=jnp.int32)[None, :]).astype(BF16)
    grad_scale = lax.rsqrt(jnp.sum(lengths).astype(F32))
    weights = jnp.concatenate([pad_hidden(w) for w in (w_gate.T, w_up.T, w_down)], axis=0)
    padded = weights.shape[0] // 3

    with jax.named_scope("gather_chips"):
        both = jnp.concatenate([inputs, upstream], axis=1)[None]
        got = exchange(copies(dense(both)[0], members // CORES), "dp", CORE_GROUPS)
        got, pick, weights, spread, grad_scale = lax.optimization_barrier(
            (got, pick, weights, spread, grad_scale)
        )
        got = undense(got, capacity).reshape(-1, 2 * features)
    with jax.named_scope("gather_core"):
        mine = jnp.dot(pick, got, preferred_element_type=F32).astype(BF16)
        other = lax.ppermute(mine, "dp", [(i, i ^ 1) for i in range(members)])
    with jax.named_scope("partial_sums"):
        kept, partial = call(
            sums_kernel,
            [
                jax.ShapeDtypeStruct(mine.shape, BF16),
                jax.ShapeDtypeStruct((shards, 3 * rows // 2, LANES), BF16),
            ],
            2 * rows * features * 3 * padded,
            mine,
            other,
            weights,
        )
    with jax.named_scope("sum_features"):
        parts = exchange(partial, "fsdp").reshape(shards, 3, rows // 2, LANES)
        gate_value, up_value, back_hidden = jnp.sum(parts.astype(F32), axis=0)
    with jax.named_scope("activation"):
        sigmoid_gate = jax.nn.sigmoid(gate_value)
        activated = gate_value * sigmoid_gate
        hidden = (activated * up_value).astype(BF16)
        grad_gate_hidden = (
            back_hidden * up_value * sigmoid_gate * (1.0 + gate_value * (1.0 - sigmoid_gate))
        ).astype(BF16)
        grad_up_hidden = (back_hidden * activated).astype(BF16)
        shard = jnp.concatenate([grad_gate_hidden, grad_up_hidden, hidden], axis=0)
    with jax.named_scope("gather_hidden"):
        gathered = exchange(copies(shard, shards), "fsdp")

    with jax.named_scope("grad_rows"):
        own, send = call(
            functools.partial(rows_kernel, 2 * heavy),
            [jax.ShapeDtypeStruct((2 * members + 2 * heavy, features), F32)] * 2,
            2 * rows * features * 2 * padded,
            core[None],
            gathered,
            weights,
            scratch=[pltpu.VMEM((rows, 2 * padded), BF16), pltpu.VMEM((rows, features), F32)],
        )
        own, send, gathered = lax.optimization_barrier((own, send, gathered))
        received = lax.ppermute(send, "dp", [(i, i ^ 1) for i in range(members)])
    with jax.named_scope("grad_weights"):
        contract_rows = (((0,), (0,)), ((), ()))
        all_hidden = gathered.reshape(padded // LANES, 2, 3, rows // 2, LANES)
        all_hidden = all_hidden.transpose(1, 3, 2, 0, 4).reshape(rows, 3 * padded)
        in_total = lax.dot_general(
            all_hidden[:, : 2 * padded],
            kept[:, :features],
            contract_rows,
            preferred_element_type=F32,
        )
        grad_in = (in_total * grad_scale).astype(BF16)
        down_total = lax.dot_general(
            all_hidden[:, 2 * padded :],
            kept[:, features:],
            contract_rows,
            preferred_element_type=F32,
        )
        grad_down = (down_total * grad_scale).astype(BF16)
        grads = (
            grad_in[:hidden_units].T,
            grad_in[padded : padded + hidden_units].T,
            grad_down[:hidden_units],
        )
        own, grads = lax.optimization_barrier((own, grads))
    with jax.named_scope("grad_rows"):
        grad_rows = (own + received).astype(BF16)
        outer = grad_rows[: 2 * members].reshape(chips, 2, 2, features)
        middle = jnp.einsum(
            "lh,htf->ltf",
            spread,
            grad_rows[2 * members :].reshape(heavy, 2, features),
            preferred_element_type=F32,
        ).astype(BF16)
        slots = jnp.stack([outer[:, 0], middle, outer[:, 1]], axis=1).reshape(chips, 6, features)
        arrived = exchange(dense(slots), "dp", CORE_GROUPS)
        grad_inputs = jnp.sum(arrived.astype(F32), axis=0, keepdims=True).astype(BF16)
        grad_inputs = undense(grad_inputs, 6)[0]

    return (grad_inputs, *grads)


def solution(mesh):
    in_specs = (
        P("dp", "fsdp"),
        P("dp", "fsdp"),
        P("fsdp", "dp"),
        P("fsdp", "dp"),
        P("dp", "fsdp"),
        P(),
        P(),
    )
    out_specs = (P("dp", "fsdp"), P("fsdp", "dp"), P("fsdp", "dp"), P("dp", "fsdp"))
    return jax.shard_map(body, mesh=mesh, in_specs=in_specs, out_specs=out_specs, check_vma=False)
```

```python
import functools

import jax
import jax.numpy as jnp
from jax import lax
from jax.experimental import pallas as pl
from jax.experimental.pallas import tpu as pltpu
from jax.sharding import PartitionSpec as P

LANES = 128
CORES = 2
BF16 = jnp.bfloat16
F32 = jnp.float32
CORE_GROUPS = [[chip * CORES + core for chip in range(32)] for core in range(CORES)]


def exchange(x, axis, groups=None):
    return lax.all_to_all(x, axis, 0, 0, tiled=True, axis_index_groups=groups)


def copies(x, count):
    return jnp.broadcast_to(x[None], (count,) + x.shape)


def dense(x):
    n, rows, columns = x.shape
    tiles = columns // LANES
    return x.reshape(n, rows, tiles, LANES).transpose(0, 2, 1, 3).reshape(n, tiles * rows, LANES)


def undense(x, rows):
    n, flat, _ = x.shape
    tiles = flat // rows
    x = x.reshape(n, tiles, rows, LANES).transpose(0, 2, 1, 3)
    return x.reshape(n, rows, tiles * LANES)


def pad_hidden(weights):
    return jnp.pad(weights, ((0, -weights.shape[0] % (4 * LANES)), (0, 0)))


def call(kernel, outs, flops, *operands, scratch=()):
    whole = pl.BlockSpec(memory_space=pltpu.VMEM)
    scalars = pl.BlockSpec(memory_space=pltpu.SMEM)
    moved = sum(x.size * x.dtype.itemsize for x in (*operands, *outs))
    return pl.pallas_call(
        kernel,
        out_shape=outs,
        in_specs=[scalars if x.ndim == 1 else whole for x in operands],
        out_specs=[whole] * len(outs),
        scratch_shapes=scratch,
        cost_estimate=pl.CostEstimate(flops=flops, bytes_accessed=moved, transcendentals=0),
        compiler_params=pltpu.CompilerParams(vmem_limit_bytes=24 * 2**20),
    )(*operands)


def sums_kernel(mine_ref, other_ref, weights_ref, kept_ref, sums_ref):
    features = weights_ref.shape[1]
    padded = weights_ref.shape[0] // 3
    half = mine_ref.shape[0] // 2
    kept_ref[...] = mine_ref[...] + other_ref[...]
    step = 2 * LANES
    for which in range(3):
        first = 0 if which < 2 else features
        for at in range(0, padded, step):
            value = lax.dot_general(
                kept_ref[:, first : first + features],
                weights_ref[which * padded + at : which * padded + at + step, :],
                (((1,), (1,)), ((), ())),
                preferred_element_type=F32,
            ).astype(BF16)
            for tile in range(step // LANES):
                for part in range(2):
                    sums_ref[
                        2 * (at // LANES + tile) + part, which * half : (which + 1) * half, :
                    ] = value[part * half : (part + 1) * half, tile * LANES : (tile + 1) * LANES]


def rows_kernel(shared, core_ref, gathered_ref, weights_ref, own_ref, send_ref, hidden_ref, all_ref):
    shards, high, _ = gathered_ref.shape
    half = high // 3
    padded = shards // 2 * LANES
    for shard in range(shards):
        tile, part = divmod(shard, 2)
        for which in range(2):
            at = which * padded + tile * LANES
            hidden_ref[part * half : (part + 1) * half, at : at + LANES] = gathered_ref[
                shard, which * half : (which + 1) * half, :
            ]
    features = weights_ref.shape[1]
    for at in range(0, features, 2 * LANES):
        to = min(at + 2 * LANES, features)
        all_ref[:, at:to] = jnp.dot(
            hidden_ref[...],
            weights_ref[: 2 * padded, at:to],
            preferred_element_type=F32,
        )
    owned = (all_ref.shape[0] - shared) // CORES
    core = core_ref[0]
    for out_ref, which in ((own_ref, core), (send_ref, 1 - core)):
        out_ref[:owned, :] = all_ref[pl.ds(pl.multiple_of(which * owned, owned), owned), :]
        out_ref[owned:, :] = all_ref[CORES * owned :, :]


def body(inputs, upstream, w_gate, w_up, w_down, lengths, move_dest):
    members = lax.axis_size("dp")
    shards = lax.axis_size("fsdp")
    core = (lax.axis_index("dp") & 1).astype(jnp.int32)
    capacity, features = inputs.shape
    hidden_units = w_gate.shape[1]
    heavy = members // 4
    rows = members * 4 + heavy * 2

    is_full = lengths == capacity
    full_rank = jnp.cumsum(is_full.astype(jnp.int32)) - is_full
    learner = jnp.arange(members, dtype=jnp.int32)[:, None]
    row = jnp.arange(capacity, dtype=jnp.int32)[None, :]
    chips = members // CORES
    first = ((learner & 1) * chips + (learner >> 1)) * 4
    target = jnp.repeat(((move_dest & 1) * chips + (move_dest >> 1)) * 4, 2, axis=1)
    target = jnp.concatenate([jnp.zeros_like(target), target], axis=1)
    place = jnp.where(
        row < 2,
        first + row,
        jnp.where(
            row < 4,
            members * 4 + full_rank[:, None] * 2 + row - 2,
            jnp.where(row < 6, first + row - 2, target + 2 + row % 2),
        ),
    )
    place = jnp.where(row < lengths[:, None], place, -1)
    place = place.reshape(-1, CORES, capacity).transpose(1, 0, 2)
    place = jnp.where(core == 0, place[0], place[1]).reshape(-1)
    pick = (jnp.arange(rows, dtype=jnp.int32)[:, None] == place[None, :]).astype(BF16)
    full = jnp.where(is_full, full_rank, -1).reshape(-1, CORES)
    full = jnp.where(core == 0, full[:, 0], full[:, 1])
    spread = (full[:, None] == jnp.arange(heavy, dtype=jnp.int32)[None, :]).astype(BF16)
    grad_scale = lax.rsqrt(jnp.sum(lengths).astype(F32))
    weights = jnp.concatenate([pad_hidden(w) for w in (w_gate.T, w_up.T, w_down)], axis=0)
    padded = weights.shape[0] // 3

    with jax.named_scope("gather_chips"):
        both = jnp.concatenate([inputs, upstream], axis=1)[None]
        got = exchange(copies(dense(both)[0], members // CORES), "dp", CORE_GROUPS)
        got, pick, weights, spread, grad_scale = lax.optimization_barrier(
            (got, pick, weights, spread, grad_scale)
        )
        got = undense(got, capacity).reshape(-1, 2 * features)
    with jax.named_scope("gather_core"):
        mine = jnp.dot(pick, got, preferred_element_type=F32).astype(BF16)
        other = lax.ppermute(mine, "dp", [(i, i ^ 1) for i in range(members)])
    with jax.named_scope("partial_sums"):
        kept, partial = call(
            sums_kernel,
            [
                jax.ShapeDtypeStruct(mine.shape, BF16),
                jax.ShapeDtypeStruct((shards, 3 * rows // 2, LANES), BF16),
            ],
            2 * rows * features * 3 * padded,
            mine,
            other,
            weights,
        )
    with jax.named_scope("sum_features"):
        parts = exchange(partial, "fsdp").reshape(shards, 3, rows // 2, LANES)
        gate_value, up_value, back_hidden = jnp.sum(parts.astype(F32), axis=0)
    with jax.named_scope("activation"):
        sigmoid_gate = jax.nn.sigmoid(gate_value)
        activated = gate_value * sigmoid_gate
        hidden = (activated * up_value).astype(BF16)
        grad_gate_hidden = (
            back_hidden * up_value * sigmoid_gate * (1.0 + gate_value * (1.0 - sigmoid_gate))
        ).astype(BF16)
        grad_up_hidden = (back_hidden * activated).astype(BF16)
        shard = jnp.concatenate([grad_gate_hidden, grad_up_hidden, hidden], axis=0)
    with jax.named_scope("gather_hidden"):
        gathered = exchange(copies(shard, shards), "fsdp")

    with jax.named_scope("grad_rows"):
        own, send = call(
            functools.partial(rows_kernel, 2 * heavy),
            [jax.ShapeDtypeStruct((2 * members + 2 * heavy, features), F32)] * 2,
            2 * rows * features * 2 * padded,
            core[None],
            gathered,
            weights,
            scratch=[pltpu.VMEM((rows, 2 * padded), BF16), pltpu.VMEM((rows, features), F32)],
        )
        grad_rows = own + lax.ppermute(send, "dp", [(i, i ^ 1) for i in range(members)])
        grad_rows = grad_rows.astype(BF16)
        outer = grad_rows[: 2 * members].reshape(chips, 2, 2, features)
        middle = jnp.einsum(
            "lh,htf->ltf",
            spread,
            grad_rows[2 * members :].reshape(heavy, 2, features),
            preferred_element_type=F32,
        ).astype(BF16)
        slots = jnp.stack([outer[:, 0], middle, outer[:, 1]], axis=1).reshape(chips, 6, features)
        message, gathered, kept = lax.optimization_barrier((dense(slots), gathered, kept))
        arrived = exchange(message, "dp", CORE_GROUPS)
        grad_inputs = jnp.sum(arrived.astype(F32), axis=0, keepdims=True).astype(BF16)
        grad_inputs = undense(grad_inputs, 6)[0]

    contract_rows = (((0,), (0,)), ((), ()))
    with jax.named_scope("grad_weights"):
        all_hidden = gathered.reshape(padded // LANES, 2, 3, rows // 2, LANES)
        all_hidden = all_hidden.transpose(1, 3, 2, 0, 4).reshape(rows, 3 * padded)
        in_total = lax.dot_general(
            all_hidden[:, : 2 * padded],
            kept[:, :features],
            contract_rows,
            preferred_element_type=F32,
        )
        grad_in = (in_total * grad_scale).astype(BF16)
        down_total = lax.dot_general(
            all_hidden[:, 2 * padded :],
            kept[:, features:],
            contract_rows,
            preferred_element_type=F32,
        )
        grad_down = (down_total * grad_scale).astype(BF16)
    return (
        grad_inputs,
        grad_in[:hidden_units].T,
        grad_in[padded : padded + hidden_units].T,
        grad_down[:hidden_units],
    )


def solution(mesh):
    in_specs = (
        P("dp", "fsdp"),
        P("dp", "fsdp"),
        P("fsdp", "dp"),
        P("fsdp", "dp"),
        P("dp", "fsdp"),
        P(),
        P(),
    )
    out_specs = (P("dp", "fsdp"), P("fsdp", "dp"), P("fsdp", "dp"), P("dp", "fsdp"))
    return jax.shard_map(body, mesh=mesh, in_specs=in_specs, out_specs=out_specs, check_vma=False)
```

```python
import functools

import jax
import jax.numpy as jnp
from jax import lax
from jax.experimental import pallas as pl
from jax.experimental.pallas import tpu as pltpu
from jax.sharding import PartitionSpec as P

LANES = 128
CORES = 2
BF16 = jnp.bfloat16
F32 = jnp.float32
CORE_GROUPS = [[chip * CORES + core for chip in range(32)] for core in range(CORES)]


def exchange(x, axis, groups=None):
    return lax.all_to_all(x, axis, 0, 0, tiled=True, axis_index_groups=groups)


def copies(x, count):
    return jnp.broadcast_to(x[None], (count,) + x.shape)


def dense(x):
    n, rows, columns = x.shape
    tiles = columns // LANES
    return x.reshape(n, rows, tiles, LANES).transpose(0, 2, 1, 3).reshape(n, tiles * rows, LANES)


def undense(x, rows):
    n, flat, _ = x.shape
    tiles = flat // rows
    x = x.reshape(n, tiles, rows, LANES).transpose(0, 2, 1, 3)
    return x.reshape(n, rows, tiles * LANES)


def pad_hidden(weights):
    return jnp.pad(weights, ((0, -weights.shape[0] % (4 * LANES)), (0, 0)))


def call(kernel, outs, flops, *operands, scratch=()):
    whole = pl.BlockSpec(memory_space=pltpu.VMEM)
    scalars = pl.BlockSpec(memory_space=pltpu.SMEM)
    moved = sum(x.size * x.dtype.itemsize for x in (*operands, *outs))
    return pl.pallas_call(
        kernel,
        out_shape=outs,
        in_specs=[scalars if x.ndim == 1 else whole for x in operands],
        out_specs=[whole] * len(outs),
        scratch_shapes=scratch,
        cost_estimate=pl.CostEstimate(flops=flops, bytes_accessed=moved, transcendentals=0),
        compiler_params=pltpu.CompilerParams(vmem_limit_bytes=24 * 2**20),
    )(*operands)


def sums_kernel(mine_ref, other_ref, weights_ref, kept_ref, sums_ref):
    features = weights_ref.shape[1]
    padded = weights_ref.shape[0] // 3
    half = mine_ref.shape[0] // 2
    kept_ref[...] = mine_ref[...] + other_ref[...]
    step = 2 * LANES
    for which in range(3):
        first = 0 if which < 2 else features
        for at in range(0, padded, step):
            value = lax.dot_general(
                kept_ref[:, first : first + features],
                weights_ref[which * padded + at : which * padded + at + step, :],
                (((1,), (1,)), ((), ())),
                preferred_element_type=F32,
            ).astype(BF16)
            for tile in range(step // LANES):
                for part in range(2):
                    sums_ref[
                        2 * (at // LANES + tile) + part, which * half : (which + 1) * half, :
                    ] = value[part * half : (part + 1) * half, tile * LANES : (tile + 1) * LANES]


def rows_kernel(shared, core_ref, gathered_ref, weights_ref, own_ref, send_ref, hidden_ref, all_ref):
    shards, high, _ = gathered_ref.shape
    half = high // 3
    padded = shards // 2 * LANES
    for shard in range(shards):
        tile, part = divmod(shard, 2)
        for which in range(3):
            at = which * padded + tile * LANES
            hidden_ref[part * half : (part + 1) * half, at : at + LANES] = gathered_ref[
                shard, which * half : (which + 1) * half, :
            ]
    features = weights_ref.shape[1]
    for at in range(0, features, 2 * LANES):
        to = min(at + 2 * LANES, features)
        all_ref[:, at:to] = jnp.dot(
            hidden_ref[:, : 2 * padded],
            weights_ref[: 2 * padded, at:to],
            preferred_element_type=F32,
        )
    owned = (all_ref.shape[0] - shared) // CORES
    core = core_ref[0]
    for out_ref, which in ((own_ref, core), (send_ref, 1 - core)):
        out_ref[:owned, :] = all_ref[pl.ds(pl.multiple_of(which * owned, owned), owned), :]
        out_ref[owned:, :] = all_ref[CORES * owned :, :]


def body(inputs, upstream, w_gate, w_up, w_down, lengths, move_dest):
    members = lax.axis_size("dp")
    shards = lax.axis_size("fsdp")
    core = (lax.axis_index("dp") & 1).astype(jnp.int32)
    capacity, features = inputs.shape
    hidden_units = w_gate.shape[1]
    heavy = members // 4
    rows = members * 4 + heavy * 2

    is_full = lengths == capacity
    full_rank = jnp.cumsum(is_full.astype(jnp.int32)) - is_full
    learner = jnp.arange(members, dtype=jnp.int32)[:, None]
    row = jnp.arange(capacity, dtype=jnp.int32)[None, :]
    chips = members // CORES
    first = ((learner & 1) * chips + (learner >> 1)) * 4
    target = jnp.repeat(((move_dest & 1) * chips + (move_dest >> 1)) * 4, 2, axis=1)
    target = jnp.concatenate([jnp.zeros_like(target), target], axis=1)
    place = jnp.where(
        row < 2,
        first + row,
        jnp.where(
            row < 4,
            members * 4 + full_rank[:, None] * 2 + row - 2,
            jnp.where(row < 6, first + row - 2, target + 2 + row % 2),
        ),
    )
    place = jnp.where(row < lengths[:, None], place, -1)
    place = place.reshape(-1, CORES, capacity).transpose(1, 0, 2)
    place = jnp.where(core == 0, place[0], place[1]).reshape(-1)
    pick = (jnp.arange(rows, dtype=jnp.int32)[:, None] == place[None, :]).astype(BF16)
    full = jnp.where(is_full, full_rank, -1).reshape(-1, CORES)
    full = jnp.where(core == 0, full[:, 0], full[:, 1])
    spread = (full[:, None] == jnp.arange(heavy, dtype=jnp.int32)[None, :]).astype(BF16)
    grad_scale = lax.rsqrt(jnp.sum(lengths).astype(F32))
    weights = jnp.concatenate([pad_hidden(w) for w in (w_gate.T, w_up.T, w_down)], axis=0)
    padded = weights.shape[0] // 3

    with jax.named_scope("gather_chips"):
        both = jnp.concatenate([inputs, upstream], axis=1)[None]
        got = exchange(copies(dense(both)[0], members // CORES), "dp", CORE_GROUPS)
        got, pick, weights, spread, grad_scale = lax.optimization_barrier(
            (got, pick, weights, spread, grad_scale)
        )
        got = undense(got, capacity).reshape(-1, 2 * features)
    with jax.named_scope("gather_core"):
        mine = jnp.dot(pick, got, preferred_element_type=F32).astype(BF16)
        other = lax.ppermute(mine, "dp", [(i, i ^ 1) for i in range(members)])
    with jax.named_scope("partial_sums"):
        kept, partial = call(
            sums_kernel,
            [
                jax.ShapeDtypeStruct(mine.shape, BF16),
                jax.ShapeDtypeStruct((shards, 3 * rows // 2, LANES), BF16),
            ],
            2 * rows * features * 3 * padded,
            mine,
            other,
            weights,
        )
    with jax.named_scope("sum_features"):
        parts = exchange(partial, "fsdp").reshape(shards, 3, rows // 2, LANES)
        gate_value, up_value, back_hidden = jnp.sum(parts.astype(F32), axis=0)
    with jax.named_scope("activation"):
        sigmoid_gate = jax.nn.sigmoid(gate_value)
        activated = gate_value * sigmoid_gate
        hidden = (activated * up_value).astype(BF16)
        grad_gate_hidden = (
            back_hidden * up_value * sigmoid_gate * (1.0 + gate_value * (1.0 - sigmoid_gate))
        ).astype(BF16)
        grad_up_hidden = (back_hidden * activated).astype(BF16)
        shard = jnp.concatenate([grad_gate_hidden, grad_up_hidden, hidden], axis=0)
    with jax.named_scope("gather_hidden"):
        gathered = exchange(copies(shard, shards), "fsdp")

    with jax.named_scope("grad_rows"):
        own, send, all_hidden = call(
            functools.partial(rows_kernel, 2 * heavy),
            [jax.ShapeDtypeStruct((2 * members + 2 * heavy, features), F32)] * 2
            + [jax.ShapeDtypeStruct((rows, 3 * padded), BF16)],
            2 * rows * features * 2 * padded,
            core[None],
            gathered,
            weights,
            scratch=[pltpu.VMEM((rows, features), F32)],
        )
        grad_rows = own + lax.ppermute(send, "dp", [(i, i ^ 1) for i in range(members)])
        grad_rows = grad_rows.astype(BF16)
        outer = grad_rows[: 2 * members].reshape(chips, 2, 2, features)
        middle = jnp.einsum(
            "lh,htf->ltf",
            spread,
            grad_rows[2 * members :].reshape(heavy, 2, features),
            preferred_element_type=F32,
        ).astype(BF16)
        slots = jnp.stack([outer[:, 0], middle, outer[:, 1]], axis=1).reshape(chips, 6, features)
        message, all_hidden, kept = lax.optimization_barrier((dense(slots), all_hidden, kept))
        arrived = exchange(message, "dp", CORE_GROUPS)
        grad_inputs = jnp.sum(arrived.astype(F32), axis=0, keepdims=True).astype(BF16)
        grad_inputs = undense(grad_inputs, 6)[0]

    contract_rows = (((0,), (0,)), ((), ()))
    with jax.named_scope("grad_weights"):
        in_total = lax.dot_general(
            all_hidden[:, : 2 * padded],
            kept[:, :features],
            contract_rows,
            preferred_element_type=F32,
        )
        grad_in = (in_total * grad_scale).astype(BF16)
        down_total = lax.dot_general(
            all_hidden[:, 2 * padded :],
            kept[:, features:],
            contract_rows,
            preferred_element_type=F32,
        )
        grad_down = (down_total * grad_scale).astype(BF16)
    return (
        grad_inputs,
        grad_in[:hidden_units].T,
        grad_in[padded : padded + hidden_units].T,
        grad_down[:hidden_units],
    )


def solution(mesh):
    in_specs = (
        P("dp", "fsdp"),
        P("dp", "fsdp"),
        P("fsdp", "dp"),
        P("fsdp", "dp"),
        P("dp", "fsdp"),
        P(),
        P(),
    )
    out_specs = (P("dp", "fsdp"), P("fsdp", "dp"), P("fsdp", "dp"), P("dp", "fsdp"))
    return jax.shard_map(body, mesh=mesh, in_specs=in_specs, out_specs=out_specs, check_vma=False)
```

```python
import functools

import jax
import jax.numpy as jnp
from jax import lax
from jax.experimental import pallas as pl
from jax.experimental.pallas import tpu as pltpu
from jax.sharding import PartitionSpec as P

LANES = 128
CORES = 2
BF16 = jnp.bfloat16
F32 = jnp.float32
CORE_GROUPS = [[chip * CORES + core for chip in range(32)] for core in range(CORES)]


def exchange(x, axis, groups=None):
    return lax.all_to_all(x, axis, 0, 0, tiled=True, axis_index_groups=groups)


def copies(x, count):
    return jnp.broadcast_to(x[None], (count,) + x.shape)


def dense(x):
    n, rows, columns = x.shape
    tiles = columns // LANES
    return x.reshape(n, rows, tiles, LANES).transpose(0, 2, 1, 3).reshape(n, tiles * rows, LANES)


def undense(x, rows):
    n, flat, _ = x.shape
    tiles = flat // rows
    x = x.reshape(n, tiles, rows, LANES).transpose(0, 2, 1, 3)
    return x.reshape(n, rows, tiles * LANES)


def pad_hidden(weights):
    return jnp.pad(weights, ((0, -weights.shape[0] % (4 * LANES)), (0, 0)))


def call(kernel, outs, flops, *operands, scratch=()):
    whole = pl.BlockSpec(memory_space=pltpu.VMEM)
    scalars = pl.BlockSpec(memory_space=pltpu.SMEM)
    moved = sum(x.size * x.dtype.itemsize for x in (*operands, *outs))
    return pl.pallas_call(
        kernel,
        out_shape=outs,
        in_specs=[scalars if x.ndim == 1 else whole for x in operands],
        out_specs=[whole] * len(outs),
        scratch_shapes=scratch,
        cost_estimate=pl.CostEstimate(flops=flops, bytes_accessed=moved, transcendentals=0),
        compiler_params=pltpu.CompilerParams(vmem_limit_bytes=24 * 2**20),
    )(*operands)


def sums_kernel(mine_ref, other_ref, weights_ref, kept_ref, sums_ref):
    features = weights_ref.shape[1]
    padded = weights_ref.shape[0] // 3
    half = mine_ref.shape[0] // 2
    kept_ref[...] = mine_ref[...] + other_ref[...]
    step = 2 * LANES
    for which in range(3):
        first = 0 if which < 2 else features
        for at in range(0, padded, step):
            value = lax.dot_general(
                kept_ref[:, first : first + features],
                weights_ref[which * padded + at : which * padded + at + step, :],
                (((1,), (1,)), ((), ())),
                preferred_element_type=F32,
            ).astype(BF16)
            for tile in range(step // LANES):
                for part in range(2):
                    sums_ref[
                        2 * (at // LANES + tile) + part, which * half : (which + 1) * half, :
                    ] = value[part * half : (part + 1) * half, tile * LANES : (tile + 1) * LANES]


def rows_kernel(shared, core_ref, gathered_ref, weights_ref, own_ref, send_ref, hidden_ref, all_ref):
    shards, high, _ = gathered_ref.shape
    half = high // 3
    padded = shards // 2 * LANES
    for shard in range(shards):
        tile, part = divmod(shard, 2)
        for which in range(3):
            at = which * padded + tile * LANES
            hidden_ref[part * half : (part + 1) * half, at : at + LANES] = gathered_ref[
                shard, which * half : (which + 1) * half, :
            ]
    features = weights_ref.shape[1]
    for at in range(0, features, 2 * LANES):
        to = min(at + 2 * LANES, features)
        all_ref[:, at:to] = jnp.dot(
            hidden_ref[:, : 2 * padded],
            weights_ref[: 2 * padded, at:to],
            preferred_element_type=F32,
        )
    owned = (all_ref.shape[0] - shared) // CORES
    core = core_ref[0]
    for out_ref, which in ((own_ref, core), (send_ref, 1 - core)):
        out_ref[:owned, :] = all_ref[pl.ds(pl.multiple_of(which * owned, owned), owned), :]
        out_ref[owned:, :] = all_ref[CORES * owned :, :]


def body(inputs, upstream, w_gate, w_up, w_down, lengths, move_dest):
    members = lax.axis_size("dp")
    shards = lax.axis_size("fsdp")
    core = (lax.axis_index("dp") & 1).astype(jnp.int32)
    capacity, features = inputs.shape
    hidden_units = w_gate.shape[1]
    heavy = members // 4
    rows = members * 4 + heavy * 2

    is_full = lengths == capacity
    full_rank = jnp.cumsum(is_full.astype(jnp.int32)) - is_full
    learner = jnp.arange(members, dtype=jnp.int32)[:, None]
    row = jnp.arange(capacity, dtype=jnp.int32)[None, :]
    chips = members // CORES
    first = ((learner & 1) * chips + (learner >> 1)) * 4
    target = jnp.repeat(((move_dest & 1) * chips + (move_dest >> 1)) * 4, 2, axis=1)
    target = jnp.concatenate([jnp.zeros_like(target), target], axis=1)
    place = jnp.where(
        row < 2,
        first + row,
        jnp.where(
            row < 4,
            members * 4 + full_rank[:, None] * 2 + row - 2,
            jnp.where(row < 6, first + row - 2, target + 2 + row % 2),
        ),
    )
    place = jnp.where(row < lengths[:, None], place, -1)
    place = place.reshape(-1, CORES, capacity).transpose(1, 0, 2)
    place = jnp.where(core == 0, place[0], place[1])
    none = jnp.full_like(place[:, 8:], -1)
    places = jnp.stack(
        [
            place[:, :8],
            jnp.concatenate([place[:, 8:], none], axis=1),
            jnp.concatenate([none, place[:, 8:]], axis=1),
        ]
    ).reshape(3, -1)
    pick = (jnp.arange(rows, dtype=jnp.int32)[None, :, None] == places[:, None, :]).astype(BF16)
    full = jnp.where(is_full, full_rank, -1).reshape(-1, CORES)
    full = jnp.where(core == 0, full[:, 0], full[:, 1])
    spread = (full[:, None] == jnp.arange(heavy, dtype=jnp.int32)[None, :]).astype(BF16)
    grad_scale = lax.rsqrt(jnp.sum(lengths).astype(F32))
    weights = jnp.concatenate([pad_hidden(w) for w in (w_gate.T, w_up.T, w_down)], axis=0)
    padded = weights.shape[0] // 3

    with jax.named_scope("gather_chips"):
        tall = jnp.concatenate([inputs[:8], upstream[:8]], axis=1)
        rest = jnp.concatenate([inputs[8:], upstream[8:]], axis=0)
        both = jnp.concatenate([dense(tall[None])[0], dense(rest[None])[0]], axis=0)
        got = exchange(copies(both, members // CORES), "dp", CORE_GROUPS)
        got, pick, weights, spread, grad_scale = lax.optimization_barrier(
            (got, pick, weights, spread, grad_scale)
        )
        cut = tall.size // LANES
        tall = undense(got[:, :cut], 8).reshape(-1, 2 * features)
        rest = undense(got[:, cut:], 8).reshape(-1, features)
    with jax.named_scope("gather_core"):
        mine = jnp.dot(pick[0], tall, preferred_element_type=F32)
        mine = mine + jnp.concatenate(
            [jnp.dot(which, rest, preferred_element_type=F32) for which in (pick[1], pick[2])],
            axis=1,
        )
        mine = mine.astype(BF16)
        other = lax.ppermute(mine, "dp", [(i, i ^ 1) for i in range(members)])
    with jax.named_scope("partial_sums"):
        kept, partial = call(
            sums_kernel,
            [
                jax.ShapeDtypeStruct(mine.shape, BF16),
                jax.ShapeDtypeStruct((shards, 3 * rows // 2, LANES), BF16),
            ],
            2 * rows * features * 3 * padded,
            mine,
            other,
            weights,
        )
    with jax.named_scope("sum_features"):
        parts = exchange(partial, "fsdp").reshape(shards, 3, rows // 2, LANES)
        gate_value, up_value, back_hidden = jnp.sum(parts.astype(F32), axis=0)
    with jax.named_scope("activation"):
        sigmoid_gate = jax.nn.sigmoid(gate_value)
        activated = gate_value * sigmoid_gate
        hidden = (activated * up_value).astype(BF16)
        grad_gate_hidden = (
            back_hidden * up_value * sigmoid_gate * (1.0 + gate_value * (1.0 - sigmoid_gate))
        ).astype(BF16)
        grad_up_hidden = (back_hidden * activated).astype(BF16)
        shard = jnp.concatenate([grad_gate_hidden, grad_up_hidden, hidden], axis=0)
    with jax.named_scope("gather_hidden"):
        gathered = exchange(copies(shard, shards), "fsdp")

    with jax.named_scope("grad_rows"):
        own, send, all_hidden = call(
            functools.partial(rows_kernel, 2 * heavy),
            [jax.ShapeDtypeStruct((2 * members + 2 * heavy, features), F32)] * 2
            + [jax.ShapeDtypeStruct((rows, 3 * padded), BF16)],
            2 * rows * features * 2 * padded,
            core[None],
            gathered,
            weights,
            scratch=[pltpu.VMEM((rows, features), F32)],
        )
        grad_rows = own + lax.ppermute(send, "dp", [(i, i ^ 1) for i in range(members)])
        grad_rows = grad_rows.astype(BF16)
        outer = grad_rows[: 2 * members].reshape(chips, 2, 2, features)
        middle = jnp.einsum(
            "lh,htf->ltf",
            spread,
            grad_rows[2 * members :].reshape(heavy, 2, features),
            preferred_element_type=F32,
        ).astype(BF16)
        slots = jnp.stack([outer[:, 0], middle, outer[:, 1]], axis=1).reshape(chips, 6, features)
        message, all_hidden, kept = lax.optimization_barrier((dense(slots), all_hidden, kept))
        arrived = exchange(message, "dp", CORE_GROUPS)
        grad_inputs = jnp.sum(arrived.astype(F32), axis=0, keepdims=True).astype(BF16)
        grad_inputs = undense(grad_inputs, 6)[0]

    contract_rows = (((0,), (0,)), ((), ()))
    with jax.named_scope("grad_weights"):
        in_total = lax.dot_general(
            all_hidden[:, : 2 * padded],
            kept[:, :features],
            contract_rows,
            preferred_element_type=F32,
        )
        grad_in = (in_total * grad_scale).astype(BF16)
        down_total = lax.dot_general(
            all_hidden[:, 2 * padded :],
            kept[:, features:],
            contract_rows,
            preferred_element_type=F32,
        )
        grad_down = (down_total * grad_scale).astype(BF16)
    return (
        grad_inputs,
        grad_in[:hidden_units].T,
        grad_in[padded : padded + hidden_units].T,
        grad_down[:hidden_units],
    )


def solution(mesh):
    in_specs = (
        P("dp", "fsdp"),
        P("dp", "fsdp"),
        P("fsdp", "dp"),
        P("fsdp", "dp"),
        P("dp", "fsdp"),
        P(),
        P(),
    )
    out_specs = (P("dp", "fsdp"), P("fsdp", "dp"), P("fsdp", "dp"), P("dp", "fsdp"))
    return jax.shard_map(body, mesh=mesh, in_specs=in_specs, out_specs=out_specs, check_vma=False)
```
